512 devices in a mesh: rep: 8 (over z_lo, core), fsdp: 64 (over y, x, z_hi).
Axes of the slice: x: 4, y: 4, z: 16 (z_hi: 4, z_lo: 4; z = z_hi * 4 + z_lo), core: 2. Of those that a mesh axis runs over, the one named last changes fastest.
Arguments:
- tokens: bfloat16 [4096, 4096], P('rep', 'fsdp'), may hold values from -6 to 6
- norm_gain: bfloat16 [4096], replicated, may hold values from 0.099609375 to 1.8984375
- gate_weight: bfloat16 [8, 5632, 4096], P('rep', 'fsdp'), may hold values from -0.09375 to 0.09375
- up_weight: bfloat16 [8, 5632, 4096], P('rep', 'fsdp'), may hold values from -0.09375 to 0.09375
- down_weight: bfloat16 [8, 5632, 4096], P('rep', 'fsdp'), may hold values from -0.09375 to 0.09375
- cotangent: bfloat16 [4096, 4096], P('rep', 'fsdp'), may hold values from -6 to 6
- outer_delta: bfloat16 [8, 5632, 4096], P('rep', 'fsdp'), may hold values from -6 to 6
- momentum: float32 [5632, 4096], P(('fsdp', 'rep')), may hold values from -6 to 6
- anchor: bfloat16 [5632, 4096], P(('fsdp', 'rep')), may hold values from -6 to 6
Outputs:
- gate_grad: bfloat16 [8, 5632, 4096], P('rep', 'fsdp')
- up_grad: bfloat16 [8, 5632, 4096], P('rep', 'fsdp')
- new_momentum: float32 [5632, 4096], P(('fsdp', 'rep'))
- new_anchor: bfloat16 [5632, 4096], P(('fsdp', 'rep'))
The draws below stay inside these ranges and needn't reach their ends.
All inputs are finite; a program needn't handle non-finite values.
Results may differ from the reference program's by a relative error of at most 0.009.
Values may be sent and summed in bfloat16 or wider, within the bound.
A program may use at most 64 MiB of HBM per device.

```python
import jax
import jax.numpy as jnp
from jax import lax

D = 4096
FFW = 5632
GROUP = 512
TOKENS = 4096
N_REP = 8


def shard_levels(stream_key, extent, shards, smallest, largest):
    def one(axis_at, shards_of):
        draws = jax.random.uniform(jax.random.fold_in(jax.random.fold_in(stream_key, 6), axis_at), (shards_of,), jnp.float32, smallest / len(shards), largest / len(shards))
        return jnp.repeat(jnp.exp(draws), extent[axis_at] // shards_of).reshape((-1,) + (1,) * (len(extent) - axis_at - 1))

    factor_of = one(*shards[0])
    for cut in shards[1:]:
        factor_of = factor_of * one(*cut)
    return factor_of


def normal_values(stream_key, extent, scale, reach, split=(), held_as=jnp.bfloat16):
    drawn = scale * jax.random.normal(stream_key, extent, jnp.float32)
    if split:
        drawn = drawn * shard_levels(stream_key, extent, split, -0.22, 0.18)
    return jnp.clip(drawn, -reach, reach).astype(held_as)


def setup_inputs(seed: int = 0) -> dict:
    key_of = jax.random.split(jax.random.key(seed), 10)
    tokens = normal_values(key_of[0], (TOKENS, D), 1.0, 6.0, ((0, 8), (1, 64)))
    norm_gain = jnp.clip(1.0 + 0.18 * jax.random.normal(key_of[1], (D,), jnp.float32), 0.099609375, 1.8984375).astype(jnp.bfloat16)
    gate_weight = normal_values(key_of[2], (N_REP, FFW, D), D ** -0.5, 0.09375, ((0, 8), (1, 64)))
    up_weight = normal_values(key_of[3], (N_REP, FFW, D), D ** -0.5, 0.09375, ((0, 8), (1, 64)))
    down_weight = normal_values(key_of[4], (N_REP, FFW, D), D ** -0.5, 0.09375, ((0, 8), (1, 64)))
    cotangent = normal_values(key_of[5], (TOKENS, D), 1.0, 6.0, ((0, 8), (1, 64)))
    outer_delta = normal_values(key_of[6], (N_REP, FFW, D), 1.0, 6.0, ((0, 8), (1, 64)))
    momentum = normal_values(key_of[7], (FFW, D), 1.0, 6.0, ((0, 512),), jnp.float32)
    anchor = normal_values(key_of[8], (FFW, D), 1.0, 6.0, ((0, 512),))
    return dict(tokens=tokens, norm_gain=norm_gain, gate_weight=gate_weight, up_weight=up_weight, down_weight=down_weight, cotangent=cotangent, outer_delta=outer_delta, momentum=momentum, anchor=anchor)


norm_epsilon = 1e-06
outer_beta = 0.9
outer_rate = 0.7

def reference(tokens, norm_gain, gate_weight, up_weight, down_weight, cotangent, outer_delta, momentum, anchor):
    values = tokens.astype(jnp.float32)
    scale = jnp.sqrt(lax.optimization_barrier(jnp.mean(values * values, axis=1, keepdims=True)) + norm_epsilon)
    normed = (values / scale * norm_gain.astype(jnp.float32)).astype(jnp.bfloat16)
    group = GROUP
    gate_list = []
    up_list = []
    for replica in range(N_REP):
        rows = normed[replica * group:(replica + 1) * group]
        upstream = cotangent[replica * group:(replica + 1) * group]
        gate_pre = jnp.dot(rows, gate_weight[replica].T, preferred_element_type=jnp.float32)
        up_pre = jnp.dot(rows, up_weight[replica].T, preferred_element_type=jnp.float32)
        back = jnp.dot(upstream, down_weight[replica].T, preferred_element_type=jnp.float32)
        sig = jax.nn.sigmoid(gate_pre)
        d_gate = (back * up_pre * sig * (1.0 + gate_pre * (1.0 - sig))).astype(jnp.bfloat16)
        d_up = (back * gate_pre * sig).astype(jnp.bfloat16)
        gate_list.append(jnp.dot(d_gate.T, rows, preferred_element_type=jnp.float32).astype(jnp.bfloat16))
        up_list.append(jnp.dot(d_up.T, rows, preferred_element_type=jnp.float32).astype(jnp.bfloat16))
    gate_grad = jnp.stack(gate_list)
    up_grad = jnp.stack(up_list)
    mean_delta = lax.optimization_barrier(jnp.sum(outer_delta.astype(jnp.float32), axis=0)) / N_REP
    new_momentum = outer_beta * momentum + mean_delta
    new_anchor = (anchor.astype(jnp.float32) - outer_rate * (mean_delta + outer_beta * new_momentum)).astype(jnp.bfloat16)
    return (gate_grad, up_grad, new_momentum, new_anchor)
```

```python
import functools

import jax
import jax.numpy as jnp
from jax import lax
from jax.experimental import pallas as pl
from jax.experimental.pallas import tpu as pltpu
from jax.sharding import PartitionSpec as P

norm_epsilon = 1e-06
outer_beta = 0.9
outer_rate = 0.7

MESH = pl.DeviceIdType.MESH
F32 = jnp.float32
BF16 = jnp.bfloat16
D = 4096
HID = 88
NT = (((1,), (1,)), ((), ()))
NN = (((1,), (0,)), ((), ()))
TOK, COT = 0, 1
GROUPS = ((0, 1), (1, 4))
TASKS = ((TOK, 0), (COT, 0), (TOK, 3), (TOK, 1), (TOK, 2), (COT, 3), (COT, 1), (COT, 2))


def kernel(
    tok_ref, cot_ref, gain_ref, gate_hbm, up_hbm, down_hbm, delta_hbm, mom_ref, anchor_ref,
    grad_gate, grad_up, new_mom, new_anchor,
    g, normed, gate_w, up_w, down_w, delta_v, gate_up, diag, acc_pre, acc_back, squares, d_t,
    share, pair_in, pair_out, line_in,
    load_sem, send, recv, zsend, zrecv, osend, orecv,
):
    f = lax.axis_index("fsdp")
    r = lax.axis_index("rep")
    y, x, zh = f // 16, (f // 4) % 4, f % 4
    zl, core = r // 2, r % 2

    def at(yy, xx, zz):
        return {"fsdp": ((yy + 4) % 4) * 16 + ((xx + 4) % 4) * 4 + (zz + 4) % 4}

    xn = (at(y, x + 1, zh), at(y, x - 1, zh))
    yn = (at(y + 1, x, zh), at(y - 1, x, zh))
    zn = (at(y, x, zh + 1), at(y, x, zh - 1))
    partner = {"rep": zl * 2 + 1 - core}
    line = [{"rep": ((zl + k) % 4) * 2 + core} for k in (1, 2, 3)]

    barrier = pltpu.get_barrier_semaphore()
    peers = [*xn, *yn, *zn, partner, *line]
    for peer in peers:
        pl.semaphore_signal(barrier, inc=1, device_id=peer, device_id_type=MESH)

    loads = [
        pltpu.make_async_copy(src, dst, load_sem.at[i])
        for i, (src, dst) in enumerate(
            ((delta_hbm, delta_v), (gate_hbm, gate_w), (up_hbm, up_w), (down_hbm, down_w))
        )
    ]
    for load in loads:
        load.start()

    def pack(t, ref):
        for h in range(2):
            top = ref[h * 256 : h * 256 + 128, :]
            bottom = ref[h * 256 + 128 : h * 256 + 256, :]
            g[t, h, 0, 0, 0] = jnp.concatenate([top, bottom], axis=1)

    pack(TOK, tok_ref)
    pack(COT, cot_ref)
    pl.semaphore_wait(barrier, len(peers))

    started, arrived = {}, set()

    def start(key, src, dst, ssem, rsem, device):
        copy = pltpu.make_async_remote_copy(
            src_ref=src, dst_ref=dst, send_sem=ssem, recv_sem=rsem,
            device_id=device, device_id_type=MESH,
        )
        copy.start()
        started[key] = copy

    def need(key):
        if key not in arrived:
            arrived.add(key)
            started[key].wait_recv()

    def xy(task, h, k, src, dst, device):
        t, rz = task
        start((task, h, k), src, dst, send.at[t, h, rz, k], recv.at[t, h, rz, k], device)

    def near(h):
        return (xn, yn) if h == 0 else (yn, xn)

    lo, hi = pl.ds(0, 64), pl.ds(64, 64)

    def first_send(task):
        for h in range(2):
            b = g.at[task[0], h, task[1]]
            xy(task, h, 0, b.at[0, 0], b.at[0, 3], near(h)[0][0])
            xy(task, h, 1, b.at[0, 0], b.at[0, 1], near(h)[0][1])

    def first_forward(task):
        for h in range(2):
            b = g.at[task[0], h, task[1]]
            need((task, h, 0))
            xy(task, h, 2, b.at[0, 3, lo], b.at[0, 2, lo], near(h)[0][0])
            need((task, h, 1))
            xy(task, h, 3, b.at[0, 1, hi], b.at[0, 2, hi], near(h)[0][1])

    def second_send(task, i):
        for h in range(2):
            b = g.at[task[0], h, task[1]]
            if i > 0:
                for k in range(4):
                    need((task, h, k))
            cols = pl.ds(GROUPS[i][0], GROUPS[i][1] - GROUPS[i][0])
            xy(task, h, 4 + 4 * i, b.at[0, cols], b.at[3, cols], near(h)[1][0])
            xy(task, h, 5 + 4 * i, b.at[0, cols], b.at[1, cols], near(h)[1][1])

    def second_forward(task, i):
        for h in range(2):
            b = g.at[task[0], h, task[1]]
            cols = pl.ds(GROUPS[i][0], GROUPS[i][1] - GROUPS[i][0])
            need((task, h, 4 + 4 * i))
            xy(task, h, 6 + 4 * i, b.at[3, cols, lo], b.at[2, cols, lo], near(h)[1][0])
            need((task, h, 5 + 4 * i))
            xy(task, h, 7 + 4 * i, b.at[1, cols, hi], b.at[2, cols, hi], near(h)[1][1])

    def z_send(t):
        for h in range(2):
            start(("z", t, h, 0), g.at[t, h, 0, 0, 0], g.at[t, h, 3, 0, 0],
                  zsend.at[t, h, 0], zrecv.at[t, h, 0], zn[0])
        for h in (1, 0):
            start(("z", t, h, 1), g.at[t, h, 0, 0, 0], g.at[t, h, 1, 0, 0],
                  zsend.at[t, h, 1], zrecv.at[t, h, 1], zn[1])

    def z_forward(t):
        need(("z", t, 0, 0))
        start(("z", t, 0, 2), g.at[t, 0, 3, 0, 0], g.at[t, 0, 2, 0, 0],
              zsend.at[t, 0, 2], zrecv.at[t, 0, 2], zn[0])
        need(("z", t, 1, 1))
        start(("z", t, 1, 2), g.at[t, 1, 1, 0, 0], g.at[t, 1, 2, 0, 0],
              zsend.at[t, 1, 2], zrecv.at[t, 1, 2], zn[1])

    def z_need(task):
        t, rz = task
        if rz:
            for h in range(2):
                need(("z", t, h, {3: 0, 1: 1, 2: 2}[rz]))

    def step_i(task):
        z_need(task)
        first_send(task)
        second_send(task, 0)

    def step_m(task):
        first_forward(task)
        second_forward(task, 0)

    def step_d(task):
        for h in range(2):
            for i in range(len(GROUPS)):
                need((task, h, 6 + 4 * i))
                need((task, h, 7 + 4 * i))

    def outer_pack():
        loads[0].wait()

        @pl.loop(0, 8)
        def _(c):
            cols = pl.ds(pl.multiple_of(c * 512, 512), 512)
            rows = delta_v[:, cols].astype(F32)
            for b in range(8):
                if b < 7:
                    block = rows[b * 11 : b * 11 + 16]
                else:
                    block = jnp.concatenate([rows[77:88], jnp.zeros((5, 512), F32)], axis=0)
                share[b % 2, b // 2, :, cols] = block.astype(BF16)

    def outer_pair():
        start("pair", share.at[1 - core], pair_in, osend.at[0], orecv.at[0], partner)

    def outer_line():
        need("pair")

        @pl.loop(0, 4)
        def _(b):
            pair_out[b] = (share[core, b].astype(F32) + pair_in[b].astype(F32)).astype(BF16)

        for k in range(3):
            start(("line", k), pair_out.at[(zl + k + 1) % 4], line_in.at[k],
                  osend.at[1 + k], orecv.at[1 + k], line[k])

    def outer_finish():
        for k in range(3):
            need(("line", k))
        total = share[core, zl].astype(F32) + pair_in[zl].astype(F32)
        for k in range(3):
            total = total + line_in[k].astype(F32)
        mean_delta = total[:11] / 8.0
        momentum = outer_beta * mom_ref[...] + mean_delta
        new_mom[...] = momentum
        new_anchor[...] = (
            anchor_ref[...].astype(F32) - outer_rate * (mean_delta + outer_beta * momentum)
        ).astype(BF16)

    low_lanes = lax.broadcasted_iota(jnp.int32, (128, 128), 1) < 64

    def prep_gate_up():
        loads[1].wait()
        loads[2].wait()

        @pl.loop(0, 8)
        def _(c):
            cols = pl.ds(pl.multiple_of(c * 512, 512), 512)
            gate_up[:, cols] = jnp.concatenate(
                [gate_w[:, cols].astype(F32), up_w[:, cols].astype(F32)], axis=0
            ).astype(BF16)

    def prep_down():
        loads[3].wait()
        low = low_lanes[:HID]

        @pl.loop(0, 16)
        def _(b):
            for pair in range(2):
                cols = pl.ds(pl.multiple_of(b * 256 + pair * 128, 128), 128)
                w = down_w[:, cols].astype(F32)
                turned = pltpu.roll(w, 64, 1)
                zero = jnp.zeros_like(w)
                diag[2 * pair, b] = jnp.concatenate(
                    [jnp.where(low, w, zero), jnp.where(low, zero, turned)], axis=0
                ).astype(BF16)
                diag[2 * pair + 1, b] = jnp.concatenate(
                    [jnp.where(low, turned, zero), jnp.where(low, zero, w)], axis=0
                ).astype(BF16)
        acc_back[...] = jnp.zeros_like(acc_back)
        acc_pre[...] = jnp.zeros_like(acc_pre)
        squares[...] = jnp.zeros_like(squares)

    def unpack(first, last):
        @pl.loop(first, last)
        def _(b):
            ry, rx = (b // 4 - y + 4) % 4, (b % 4 - x + 4) % 4
            for h in range(2):
                parts = [
                    g[TOK, h, (zs - zh + 4) % 4, ry if h == 0 else rx, rx if h == 0 else ry].astype(F32)
                    for zs in range(4)
                ]
                for pair in range(2):
                    even, odd = parts[2 * pair], parts[2 * pair + 1]
                    top = jnp.where(low_lanes, even, pltpu.roll(odd, 64, 1))
                    bottom = jnp.where(low_lanes, pltpu.roll(even, 64, 1), odd)
                    cols = pl.ds(pl.multiple_of(b * 256 + pair * 128, 128), 128)
                    for i, block in enumerate((top, bottom)):
                        rows = pl.ds(h * 256 + i * 128, 128)
                        normed[rows, cols] = block.astype(BF16)
                        squares[rows, :] += block * block

    def inverse_scale():
        total = jnp.sum(squares[...], axis=1, keepdims=True)
        squares[...] = jnp.broadcast_to(
            1.0 / jnp.sqrt(total / D + norm_epsilon), squares.shape
        )

    def forward(first, last):
        @pl.loop(first, last)
        def _(b):
            cols = pl.ds(pl.multiple_of(b * 256, 256), 256)
            gain = gain_ref[:, cols].astype(F32)
            scale = squares[...]
            scale = jnp.concatenate([scale, scale], axis=1)
            block = (normed[:, cols].astype(F32) * scale * gain).astype(BF16)
            normed[:, cols] = block
            acc_pre[...] += lax.dot_general(
                gate_up[:, cols], block, NT, preferred_element_type=F32
            )

    def backward(task):
        step_d(task)
        rz = task[1]
        zs = (zh + rz) % 4

        @pl.loop(0, 4)
        def _(ry):
            ws, rows = [], []
            for rx in range(4):
                ws.append(diag[zs, ((y + ry) % 4) * 4 + (x + rx) % 4])
            for h in range(2):
                rows.append(
                    jnp.concatenate(
                        [
                            g[COT, h, rz, ry if h == 0 else rx, rx if h == 0 else ry]
                            for rx in range(4)
                        ],
                        axis=1,
                    )
                )
            acc_back[...] += lax.dot_general(
                jnp.concatenate(ws, axis=1), jnp.concatenate(rows, axis=0), NT,
                preferred_element_type=F32,
            )

    def finish():
        for q in range(4):
            lanes = pl.ds(q * 128, 128)
            gate_pre = acc_pre[:HID, lanes]
            up_pre = acc_pre[HID:, lanes]
            half = pl.ds((q // 2) * 128, 128)
            back = acc_back[HID * (q % 2) : HID * (q % 2) + HID, half]
            sig = jax.nn.sigmoid(gate_pre)
            d_gate = back * up_pre * sig * (1.0 + gate_pre * (1.0 - sig))
            d_up = back * gate_pre * sig
            d_t[:, lanes] = jnp.concatenate([d_gate, d_up], axis=0).astype(BF16)

        @pl.loop(0, 8)
        def _(c):
            cols = pl.ds(pl.multiple_of(c * 512, 512), 512)
            out = lax.dot_general(d_t[...], normed[:, cols], NN, preferred_element_type=F32)
            grad_gate[:, cols] = out[:HID].astype(BF16)
            grad_up[:, cols] = out[HID:].astype(BF16)

    T = TASKS
    n = len(T)
    z_send(TOK)
    step_i(T[0])
    step_i(T[1])
    z_send(COT)
    outer_pack()
    outer_pair()
    step_m(T[0])
    work = {
        0: [prep_gate_up, lambda: z_forward(TOK)],
        1: [prep_down],
        2: [lambda: z_forward(COT)],
        3: [outer_line, lambda: backward(T[1])],
        6: [lambda: step_d(T[0]), lambda: step_d(T[2]), lambda: step_d(T[3]), lambda: step_d(T[4]), lambda: unpack(0, 16)],
        7: [inverse_scale, lambda: forward(0, 16), outer_finish],
        8: [lambda: backward(T[5])],
        9: [lambda: backward(T[6])],
    }
    for i in range(n + 2):
        if i < n:
            second_send(T[i], 1)
        if i + 1 < n:
            step_m(T[i + 1])
        if i + 2 < n:
            step_i(T[i + 2])
        if 0 <= i - 1 < n:
            second_forward(T[i - 1], 1)
        for piece in work.get(i, ()):
            piece()
    backward(T[7])
    for key, copy in started.items():
        if key not in arrived:
            need(key)
        copy.wait_send()
    finish()


def body(
    tokens, norm_gain, gate_weight, up_weight, down_weight, cotangent, outer_delta, momentum, anchor
):
    vmem = pl.BlockSpec(memory_space=pltpu.VMEM)
    hbm = pl.BlockSpec(memory_space=pl.ANY)
    nk = 4 + 4 * len(GROUPS)
    dma = pltpu.SemaphoreType.DMA
    outs = pl.pallas_call(
        kernel,
        out_shape=(
            jax.ShapeDtypeStruct((HID, D), BF16),
            jax.ShapeDtypeStruct((HID, D), BF16),
            jax.ShapeDtypeStruct((11, D), F32),
            jax.ShapeDtypeStruct((11, D), BF16),
        ),
        in_specs=[vmem, vmem, vmem, hbm, hbm, hbm, hbm, vmem, vmem],
        out_specs=(vmem, vmem, vmem, vmem),
        scratch_shapes=[
            pltpu.VMEM((2, 2, 4, 4, 4, 128, 128), BF16),
            pltpu.VMEM((512, D), BF16),
            pltpu.VMEM((HID, D), BF16),
            pltpu.VMEM((HID, D), BF16),
            pltpu.VMEM((HID, D), BF16),
            pltpu.VMEM((HID, D), BF16),
            pltpu.VMEM((2 * HID, D), BF16),
            pltpu.VMEM((4, 16, 2 * HID, 128), BF16),
            pltpu.VMEM((2 * HID, 512), F32),
            pltpu.VMEM((2 * HID, 256), F32),
            pltpu.VMEM((512, 128), F32),
            pltpu.VMEM((2 * HID, 512), BF16),
            pltpu.VMEM((2, 4, 16, D), BF16),
            pltpu.VMEM((4, 16, D), BF16),
            pltpu.VMEM((4, 16, D), BF16),
            pltpu.VMEM((3, 16, D), BF16),
            dma((4,)),
            dma((2, 2, 4, nk)),
            dma((2, 2, 4, nk)),
            dma((2, 2, 3)),
            dma((2, 2, 3)),
            dma((4,)),
            dma((4,)),
        ],
        compiler_params=pltpu.CompilerParams(
            collective_id=0, has_side_effects=True, vmem_limit_bytes=48 * 2**20
        ),
        cost_estimate=pl.CostEstimate(
            flops=10 * 512 * D * HID, bytes_accessed=8 * 2**20, transcendentals=512 * HID
        ),
        name="gather_and_grads",
    )(
        tokens, cotangent, norm_gain.reshape(1, D), gate_weight[0], up_weight[0], down_weight[0],
        outer_delta[0], momentum, anchor,
    )
    return outs[0][None], outs[1][None], outs[2], outs[3]


def solution(mesh):
    return jax.shard_map(
        body,
        mesh=mesh,
        in_specs=(
            P("rep", "fsdp"),
            P(),
            P("rep", "fsdp", None),
            P("rep", "fsdp", None),
            P("rep", "fsdp", None),
            P("rep", "fsdp"),
            P("rep", "fsdp", None),
            P(("fsdp", "rep"), None),
            P(("fsdp", "rep"), None),
        ),
        out_specs=(
            P("rep", "fsdp", None),
            P("rep", "fsdp", None),
            P(("fsdp", "rep"), None),
            P(("fsdp", "rep"), None),
        ),
        check_vma=False,
    )
```

```python
import functools

import jax
import jax.numpy as jnp
from jax import lax
from jax.experimental import pallas as pl
from jax.experimental.pallas import tpu as pltpu
from jax.sharding import PartitionSpec as P

norm_epsilon = 1e-06
outer_beta = 0.9
outer_rate = 0.7

MESH = pl.DeviceIdType.MESH
F32 = jnp.float32
BF16 = jnp.bfloat16
D = 4096
HID = 88
NT = (((1,), (1,)), ((), ()))
NN = (((1,), (0,)), ((), ()))
TOK, COT = 0, 1
ORDER = (
    ('F', 0, 0), ('Z', 0), ('PG',), ('S', 1, 0, 0), ('F', 1, 0), ('S', 0, 0, 0), ('Z', 1), ('FF', 0, 0),
    ('FF', 1, 0), ('OP',), ('SF', 0, 0, 0), ('SF', 1, 0, 0), ('S', 0, 0, 1), ('S', 1, 0, 1), ('ZF', 0),
    ('F', 0, 1), ('F', 0, 3), ('S', 0, 1, 0), ('S', 0, 3, 0), ('PU',), ('SF', 0, 0, 1), ('SF', 1, 0, 1),
    ('FF', 0, 3), ('SF', 0, 1, 0), ('FF', 0, 1), ('ZF', 1), ('SF', 0, 3, 0), ('S', 1, 3, 0), ('F', 1, 1),
    ('F', 1, 3), ('S', 0, 3, 1), ('F', 0, 2), ('S', 0, 2, 0), ('OL',), ('FF', 1, 1), ('FF', 1, 3),
    ('S', 0, 1, 1), ('F', 1, 2), ('FF', 0, 2), ('PD',), ('S', 1, 3, 1), ('SF', 0, 3, 1), ('S', 0, 2, 1),
    ('SF', 0, 2, 0), ('SQ', 0, 0), ('FF', 1, 2), ('S', 1, 1, 0), ('S', 1, 1, 1), ('SF', 0, 1, 1),
    ('BW', 1, 0), ('SQ', 0, 3), ('SF', 0, 2, 1), ('S', 1, 2, 0), ('S', 1, 2, 1), ('SF', 1, 1, 0),
    ('SF', 1, 1, 1), ('OF',), ('SF', 1, 3, 1), ('SF', 1, 3, 0), ('SQ', 0, 1), ('SQ', 0, 2), ('FW', 0),
    ('SF', 1, 2, 0), ('FW', 1), ('SF', 1, 2, 1), ('FW', 2), ('BW', 1, 1), ('FW', 3), ('BW', 1, 3),
    ('BW', 1, 2),
)
GROUPS = {
    (0, 0): ((0, 1), (1, 4)),
    (1, 0): ((0, 1), (1, 4)),
    (0, 3): ((0, 1), (1, 4)),
    (0, 1): ((0, 1), (1, 4)),
    (1, 3): ((0, 1), (1, 4)),
    (0, 2): ((0, 1), (1, 4)),
    (1, 1): ((0, 1), (1, 4)),
    (1, 2): ((0, 1), (1, 4)),
}
COPIES = 4 + 4 * max(len(groups) for groups in GROUPS.values())


def kernel(
    tok_hbm, cot_hbm, gain_ref, gate_hbm, up_hbm, down_hbm, delta_hbm,
    d_out, normed_out, total_out,
    g, normed, gate_w, up_w, down_w, delta_v, gate_up, down_z, acc_pre, acc_back, squares, gain_v,
    share, pair_in, pair_out, line_in,
    load_sem, own_sem, out_sem, send, recv, zsend, zrecv, osend, orecv,
):
    f = lax.axis_index("fsdp")
    r = lax.axis_index("rep")
    y, x, zh = f // 16, (f // 4) % 4, f % 4
    zl, core = r // 2, r % 2

    def at(yy, xx, zz):
        return {"fsdp": ((yy + 4) % 4) * 16 + ((xx + 4) % 4) * 4 + (zz + 4) % 4}

    xn = (at(y, x + 1, zh), at(y, x - 1, zh))
    yn = (at(y + 1, x, zh), at(y - 1, x, zh))
    zn = (at(y, x, zh + 1), at(y, x, zh - 1))
    partner = {"rep": zl * 2 + 1 - core}
    line = [{"rep": ((zl + k) % 4) * 2 + core} for k in (1, 2, 3)]

    own = [
        pltpu.make_async_copy(ref.at[:, pl.ds(256 * h, 256)], g.at[t, h, 0, 0, 0], own_sem.at[t, h])
        for t, ref in ((TOK, tok_hbm), (COT, cot_hbm))
        for h in range(2)
    ]
    loads = [
        pltpu.make_async_copy(src, dst, load_sem.at[i])
        for i, (src, dst) in enumerate(
            ((delta_hbm, delta_v), (gate_hbm, gate_w), (up_hbm, up_w), (down_hbm, down_w))
        )
    ]
    for load in own:
        load.start()
    barrier = pltpu.get_barrier_semaphore()
    peers = [*zn, *line, partner, *xn, *yn]
    for peer in peers:
        pl.semaphore_signal(barrier, inc=1, device_id=peer, device_id_type=MESH)
    for load in own:
        load.wait()
    pl.semaphore_wait(barrier, len(peers))

    started, arrived = {}, set()

    def start(key, src, dst, ssem, rsem, device):
        copy = pltpu.make_async_remote_copy(
            src_ref=src, dst_ref=dst, send_sem=ssem, recv_sem=rsem,
            device_id=device, device_id_type=MESH,
        )
        copy.start()
        started[key] = copy

    def need(key):
        if key not in arrived:
            arrived.add(key)
            started[key].wait_recv()

    def xy(task, h, k, src, dst, device):
        t, rz = task
        start((task, h, k), src, dst, send.at[t, h, rz, k], recv.at[t, h, rz, k], device)

    def near(h):
        return (xn, yn) if h == 0 else (yn, xn)

    lo, hi = pl.ds(0, 32), pl.ds(32, 32)

    def first_send(task):
        for h in range(2):
            b = g.at[task[0], h, task[1]]
            xy(task, h, 0, b.at[0, 0], b.at[0, 3], near(h)[0][0])
            xy(task, h, 1, b.at[0, 0], b.at[0, 1], near(h)[0][1])

    def first_forward(task):
        for h in range(2):
            b = g.at[task[0], h, task[1]]
            need((task, h, 0))
            xy(task, h, 2, b.at[0, 3, lo], b.at[0, 2, lo], near(h)[0][0])
            need((task, h, 1))
            xy(task, h, 3, b.at[0, 1, hi], b.at[0, 2, hi], near(h)[0][1])

    brings = {0: (), 1: (1,), 2: (2, 3), 3: (0,)}

    def second_send(task, i):
        first, last = GROUPS[task][i]
        for h in range(2):
            b = g.at[task[0], h, task[1]]
            for offset in range(first, last):
                for k in brings[offset]:
                    need((task, h, k))
            cols = pl.ds(first, last - first)
            xy(task, h, 4 + 4 * i, b.at[0, cols], b.at[3, cols], near(h)[1][0])
            xy(task, h, 5 + 4 * i, b.at[0, cols], b.at[1, cols], near(h)[1][1])

    def second_forward(task, i):
        first, last = GROUPS[task][i]
        for h in range(2):
            b = g.at[task[0], h, task[1]]
            cols = pl.ds(first, last - first)
            need((task, h, 4 + 4 * i))
            xy(task, h, 6 + 4 * i, b.at[3, cols, lo], b.at[2, cols, lo], near(h)[1][0])
            need((task, h, 5 + 4 * i))
            xy(task, h, 7 + 4 * i, b.at[1, cols, hi], b.at[2, cols, hi], near(h)[1][1])

    def z_send(t):
        for h in range(2):
            start(("z", t, h, 0), g.at[t, h, 0, 0, 0], g.at[t, h, 3, 0, 0],
                  zsend.at[t, h, 0], zrecv.at[t, h, 0], zn[0])
        for h in (1, 0):
            start(("z", t, h, 1), g.at[t, h, 0, 0, 0], g.at[t, h, 1, 0, 0],
                  zsend.at[t, h, 1], zrecv.at[t, h, 1], zn[1])

    def z_forward(t):
        need(("z", t, 0, 0))
        start(("z", t, 0, 2), g.at[t, 0, 3, 0, 0], g.at[t, 0, 2, 0, 0],
              zsend.at[t, 0, 2], zrecv.at[t, 0, 2], zn[0])
        need(("z", t, 1, 1))
        start(("z", t, 1, 2), g.at[t, 1, 1, 0, 0], g.at[t, 1, 2, 0, 0],
              zsend.at[t, 1, 2], zrecv.at[t, 1, 2], zn[1])

    def z_need(task):
        t, rz = task
        if rz:
            for h in range(2):
                need(("z", t, h, {3: 0, 1: 1, 2: 2}[rz]))

    sent = set()

    def arrive(task):
        for h in range(2):
            for i in range(len(GROUPS[task])):
                need((task, h, 6 + 4 * i))
                need((task, h, 7 + 4 * i))
        for key, copy in started.items():
            if key[0] == task and key not in sent:
                sent.add(key)
                copy.wait_send()

    def outer_pack():
        loads[0].wait()

        @pl.loop(0, 8)
        def _(c):
            cols = pl.ds(pl.multiple_of(c * 512, 512), 512)
            rows = delta_v[:, cols].astype(F32)
            for b in range(8):
                if b < 7:
                    block = rows[b * 11 : b * 11 + 16]
                else:
                    block = jnp.concatenate([rows[77:88], jnp.zeros((5, 512), F32)], axis=0)
                share[b % 2, b // 2, :, cols] = block.astype(BF16)

    def outer_pair():
        start("pair", share.at[1 - core], pair_in, osend.at[0], orecv.at[0], partner)

    def outer_line():
        need("pair")

        @pl.loop(0, 4)
        def _(b):
            pair_out[b] = (share[core, b].astype(F32) + pair_in[b].astype(F32)).astype(BF16)

        for k in range(3):
            start(("line", k), pair_out.at[(zl + k + 1) % 4], line_in.at[k],
                  osend.at[1 + k], orecv.at[1 + k], line[k])

    def outer_finish():
        for k in range(3):
            need(("line", k))
        total = share[core, zl].astype(F32) + pair_in[zl].astype(F32)
        for k in range(3):
            total = total + line_in[k].astype(F32)
        total_out[...] = total

    def prep_gate_up():
        loads[1].wait()
        loads[2].wait()

        @pl.loop(0, 8)
        def _(c):
            cols = pl.ds(pl.multiple_of(c * 512, 512), 512)
            gate_up[:, cols] = jnp.concatenate(
                [gate_w[:, cols].astype(F32), up_w[:, cols].astype(F32)], axis=0
            ).astype(BF16)

    def prep_gain():
        @pl.loop(0, 16)
        def _(c):
            cols = pl.ds(pl.multiple_of(c * 256, 256), 256)
            row = gain_ref[cols].astype(F32)
            gain_v[cols, :] = jnp.broadcast_to(row[None, :], (128, 256)).T

        acc_back[...] = jnp.zeros_like(acc_back)
        acc_pre[...] = jnp.zeros_like(acc_pre)
        squares[...] = jnp.zeros_like(squares)

    def prep_down():
        loads[3].wait()
        low = lax.broadcasted_iota(jnp.int32, (HID, 128), 1) < 64

        @pl.loop(0, 4)
        def _(yy):
            for pair in range(2):
                for xs in range(2):
                    a, b = (
                        down_w[
                            :, pl.ds(pl.multiple_of((yy * 4 + xx) * 256 + pair * 128, 128), 128)
                        ].astype(F32)
                        for xx in (2 * xs, 2 * xs + 1)
                    )
                    lanes = pl.ds(xs * 128, 128)
                    down_z[2 * pair, yy, :, lanes] = jnp.where(low, a, pltpu.roll(b, 64, 1)).astype(BF16)
                    down_z[2 * pair + 1, yy, :, lanes] = jnp.where(low, pltpu.roll(a, 64, 1), b).astype(BF16)

    def block_of(t, rz, ry, rx):
        return jnp.concatenate([g[t, 0, rz, ry, rx], g[t, 1, rz, rx, ry]], axis=1)

    def add_squares(task):
        arrive(task)

        @pl.loop(0, 16)
        def _(b):
            v = block_of(TOK, task[1], b // 4, b % 4).astype(F32)
            v = v * v
            part = v[:8]
            for i in range(1, 8):
                part = part + v[8 * i : 8 * i + 8]
            squares[...] += part

    def inverse_scale():
        total = jnp.sum(squares[...], axis=0, keepdims=True)
        squares[...] = jnp.broadcast_to(1.0 / jnp.sqrt(total / D + norm_epsilon), squares.shape)

    def normed_copy(b):
        rows = pl.ds(pl.multiple_of(b * 256, 256), 256)
        return pltpu.make_async_copy(normed.at[rows], normed_out.at[rows], out_sem.at[b])

    def forward(first, last):
        @pl.loop(first, last)
        def _(b):
            ry, rx = (b // 4 - y + 4) % 4, (b % 4 - x + 4) % 4
            cols = pl.ds(pl.multiple_of(b * 256, 256), 256)
            scale = squares[0:1, :]
            gain = gain_v[cols, :]
            gain = jnp.concatenate([gain] * 4, axis=1)
            raw = jnp.concatenate(
                [block_of(TOK, (zs - zh + 4) % 4, ry, rx) for zs in range(4)], axis=0
            )
            block = (raw.astype(F32) * scale * gain).astype(BF16)
            normed[cols, :] = block
            normed_copy(b).start()
            acc_pre[...] += lax.dot_general(
                gate_up[:, cols], block, NN, preferred_element_type=F32
            )

    def backward(task):
        arrive(task)
        rz = task[1]
        zs = (zh + rz) % 4

        @pl.loop(0, 4)
        def _(yy):
            ry = (yy - y + 4) % 4
            rows = jnp.concatenate(
                [block_of(COT, rz, ry, (xx - x + 4) % 4) for xx in range(4)], axis=0
            )
            acc_back[...] += lax.dot_general(
                down_z[zs, yy], rows, NN, preferred_element_type=F32
            )

    def finish():
        for q in range(4):
            lanes = pl.ds(q * 128, 128)
            gate_pre = acc_pre[:HID, lanes]
            up_pre = acc_pre[HID:, lanes]
            back = acc_back[:, lanes]
            sig = jax.nn.sigmoid(gate_pre)
            d_gate = back * up_pre * sig * (1.0 + gate_pre * (1.0 - sig))
            d_up = back * gate_pre * sig
            d_out[:, lanes] = jnp.concatenate([d_gate, d_up], axis=0).astype(BF16)

    def run(op):
        name, args = op[0], op[1:]
        task = args[:2]
        if name == "Z":
            z_send(args[0])
        elif name == "ZF":
            z_forward(args[0])
        elif name == "F":
            z_need(task)
            first_send(task)
        elif name == "FF":
            first_forward(task)
        elif name == "S":
            z_need(task)
            second_send(task, args[2])
        elif name == "SF":
            second_forward(task, args[2])
        elif name == "OP":
            outer_pack()
            outer_pair()
        elif name == "OL":
            outer_line()
        elif name == "OF":
            outer_finish()
        elif name == "PG":
            prep_gain()
        elif name == "PD":
            prep_down()
        elif name == "PU":
            prep_gate_up()
        elif name == "SQ":
            add_squares(task)
        elif name == "FW":
            if args[0] == 0:
                inverse_scale()
            forward(4 * args[0], 4 * args[0] + 4)
        elif name == "BW":
            backward(task)

    for i, op in enumerate(ORDER):
        if i == 3:
            for load in loads:
                load.start()
        run(op)
    finish()
    for b in range(16):
        normed_copy(b).wait()
    for key, copy in started.items():
        if key not in sent:
            copy.wait_send()


CHUNKS = 8


def finish_kernel(
    d_ref, normed_hbm, total_ref, mom_ref, anchor_ref,
    grad_gate, grad_up, new_mom, new_anchor,
    normed, gate_v, up_v, in_sem, out_sem,
):
    wide = D // CHUNKS
    reads = [
        pltpu.make_async_copy(
            normed_hbm.at[pl.ds(c * wide, wide)], normed.at[pl.ds(c * wide, wide)], in_sem.at[c]
        )
        for c in range(CHUNKS)
    ]
    for read in reads:
        read.start()
    mean_delta = total_ref[:11] / 8.0
    momentum = outer_beta * mom_ref[...] + mean_delta
    new_mom[...] = momentum
    new_anchor[...] = (
        anchor_ref[...].astype(F32) - outer_rate * (mean_delta + outer_beta * momentum)
    ).astype(BF16)
    writes = []
    for c in range(CHUNKS):
        cols = pl.ds(c * wide, wide)
        reads[c].wait()
        out = lax.dot_general(d_ref[...], normed[cols, :], NT, preferred_element_type=F32)
        gate_v[:, cols] = out[:HID].astype(BF16)
        up_v[:, cols] = out[HID:].astype(BF16)
        for i, (src, dst) in enumerate(((gate_v, grad_gate), (up_v, grad_up))):
            writes.append(
                pltpu.make_async_copy(src.at[:, cols], dst.at[:, cols], out_sem.at[c, i])
            )
            writes[-1].start()
    for write in writes:
        write.wait()


def body(
    tokens, norm_gain, gate_weight, up_weight, down_weight, cotangent, outer_delta, momentum, anchor
):
    vmem = pl.BlockSpec(memory_space=pltpu.VMEM)
    hbm = pl.BlockSpec(memory_space=pltpu.HBM)
    dma = pltpu.SemaphoreType.DMA
    d_t, normed, total = pl.pallas_call(
        kernel,
        out_shape=(
            jax.ShapeDtypeStruct((2 * HID, 512), BF16),
            jax.ShapeDtypeStruct((D, 512), BF16),
            jax.ShapeDtypeStruct((16, D), F32),
        ),
        in_specs=[hbm, hbm, vmem, hbm, hbm, hbm, hbm],
        out_specs=(vmem, hbm, vmem),
        scratch_shapes=[
            pltpu.VMEM((2, 2, 4, 4, 4, 64, 256), BF16),
            pltpu.VMEM((D, 512), BF16),
            pltpu.VMEM((HID, D), BF16),
            pltpu.VMEM((HID, D), BF16),
            pltpu.VMEM((HID, D), BF16),
            pltpu.VMEM((HID, D), BF16),
            pltpu.VMEM((2 * HID, D), BF16),
            pltpu.VMEM((4, 4, HID, 256), BF16),
            pltpu.VMEM((2 * HID, 512), F32),
            pltpu.VMEM((HID, 512), F32),
            pltpu.VMEM((8, 512), F32),
            pltpu.VMEM((D, 128), F32),
            pltpu.VMEM((2, 4, 16, D), BF16),
            pltpu.VMEM((4, 16, D), BF16),
            pltpu.VMEM((4, 16, D), BF16),
            pltpu.VMEM((3, 16, D), BF16),
            dma((4,)),
            dma((2, 2)),
            dma((16,)),
            dma((2, 2, 4, COPIES)),
            dma((2, 2, 4, COPIES)),
            dma((2, 2, 3)),
            dma((2, 2, 3)),
            dma((4,)),
            dma((4,)),
        ],
        compiler_params=pltpu.CompilerParams(
            collective_id=0, has_side_effects=True, vmem_limit_bytes=62 * 2**20
        ),
        cost_estimate=pl.CostEstimate(
            flops=6 * 512 * D * HID, bytes_accessed=8 * 2**20, transcendentals=512 * HID
        ),
        name="gather_and_forward",
    )(
        tokens.T, cotangent.T, norm_gain, gate_weight[0], up_weight[0], down_weight[0],
        outer_delta[0],
    )
    outs = pl.pallas_call(
        finish_kernel,
        out_shape=(
            jax.ShapeDtypeStruct((HID, D), BF16),
            jax.ShapeDtypeStruct((HID, D), BF16),
            jax.ShapeDtypeStruct((11, D), F32),
            jax.ShapeDtypeStruct((11, D), BF16),
        ),
        in_specs=[vmem, hbm, vmem, vmem, vmem],
        out_specs=(hbm, hbm, vmem, vmem),
        scratch_shapes=[
            pltpu.VMEM((D, 512), BF16),
            pltpu.VMEM((HID, D), BF16),
            pltpu.VMEM((HID, D), BF16),
            dma((CHUNKS,)),
            dma((CHUNKS, 2)),
        ],
        compiler_params=pltpu.CompilerParams(vmem_limit_bytes=62 * 2**20),
        cost_estimate=pl.CostEstimate(
            flops=4 * 512 * D * HID, bytes_accessed=6 * 2**20, transcendentals=0
        ),
        name="gradients_and_outer_update",
    )(d_t, normed, total, momentum, anchor)
    return outs[0][None], outs[1][None], outs[2], outs[3]


def solution(mesh):
    return jax.shard_map(
        body,
        mesh=mesh,
        in_specs=(
            P("rep", "fsdp"),
            P(),
            P("rep", "fsdp", None),
            P("rep", "fsdp", None),
            P("rep", "fsdp", None),
            P("rep", "fsdp"),
            P("rep", "fsdp", None),
            P(("fsdp", "rep"), None),
            P(("fsdp", "rep"), None),
        ),
        out_specs=(
            P("rep", "fsdp", None),
            P("rep", "fsdp", None),
            P(("fsdp", "rep"), None),
            P(("fsdp", "rep"), None),
        ),
        check_vma=False,
    )
```

```python
import functools

import jax
import jax.numpy as jnp
from jax import lax
from jax.experimental import pallas as pl
from jax.experimental.pallas import tpu as pltpu
from jax.sharding import PartitionSpec as P

norm_epsilon = 1e-06
outer_beta = 0.9
outer_rate = 0.7

MESH = pl.DeviceIdType.MESH
F32 = jnp.float32
BF16 = jnp.bfloat16
D = 4096
HID = 88
NT = (((1,), (1,)), ((), ()))
NN = (((1,), (0,)), ((), ()))
TOK, COT = 0, 1
ORDER = (
    ('F', 1, 0), ('Z', 0), ('S', 1, 0, 0), ('F', 0, 0), ('S', 0, 0, 0), ('FF', 1, 0), ('FF', 0, 0), ('PG',),
    ('Z', 1), ('SF', 0, 0, 0), ('SF', 1, 0, 0), ('S', 1, 0, 1), ('S', 0, 0, 1), ('PD',), ('S', 0, 1, 0),
    ('ZF', 0), ('F', 0, 1), ('S', 0, 3, 0), ('SF', 1, 0, 1), ('F', 0, 3), ('SF', 0, 0, 1), ('SF', 0, 1, 0),
    ('ZF', 1), ('SF', 0, 3, 0), ('FF', 0, 1), ('F', 1, 3), ('OP',), ('F', 1, 1), ('S', 1, 3, 0),
    ('S', 1, 1, 0), ('FF', 0, 3), ('S', 0, 2, 0), ('F', 0, 2), ('S', 0, 1, 1), ('OL',), ('S', 0, 3, 1),
    ('FF', 0, 2), ('FF', 1, 1), ('F', 1, 2), ('SF', 0, 2, 0), ('FF', 1, 3), ('S', 1, 2, 0), ('SF', 0, 1, 1),
    ('BW', 1, 0), ('S', 0, 2, 1), ('SF', 0, 3, 1), ('FF', 1, 2), ('SQ', 0, 0), ('PU',), ('S', 1, 1, 1),
    ('SF', 0, 2, 1), ('S', 1, 3, 1), ('S', 1, 2, 1), ('SQ', 0, 1), ('SQ', 0, 3), ('SF', 1, 1, 0),
    ('SF', 1, 2, 0), ('SQ', 0, 2), ('SF', 1, 1, 1), ('SF', 1, 3, 0), ('FW', 0), ('FW', 1), ('SF', 1, 3, 1),
    ('SF', 1, 2, 1), ('FW', 2), ('FW', 3), ('OF',), ('BW', 1, 1), ('BW', 1, 3), ('BW', 1, 2),
)
GROUPS = {
    (0, 0): ((0, 1), (1, 4)),
    (1, 0): ((0, 1), (1, 4)),
    (0, 3): ((0, 1), (1, 4)),
    (0, 1): ((0, 1), (1, 4)),
    (1, 3): ((0, 1), (1, 4)),
    (0, 2): ((0, 1), (1, 4)),
    (1, 1): ((0, 1), (1, 4)),
    (1, 2): ((0, 1), (1, 4)),
}
COPIES = 4 + 4 * max(len(groups) for groups in GROUPS.values())


def kernel(
    tok_hbm, cot_hbm, gain_hbm, gate_hbm, up_hbm, down_hbm, delta_hbm,
    d_out, normed, total_out,
    g, gate_w, up_w, down_w, delta_v, gate_up, down_z, acc_pre, acc_back, squares, gain_v, gain_ref,
    share, pair_in, pair_out, line_in,
    load_sem, own_sem, send, recv, zsend, zrecv, osend, orecv,
):
    f = lax.axis_index("fsdp")
    r = lax.axis_index("rep")
    y, x, zh = f // 16, (f // 4) % 4, f % 4
    zl, core = r // 2, r % 2

    def at(yy, xx, zz):
        return {"fsdp": ((yy + 4) % 4) * 16 + ((xx + 4) % 4) * 4 + (zz + 4) % 4}

    xn = (at(y, x + 1, zh), at(y, x - 1, zh))
    yn = (at(y + 1, x, zh), at(y - 1, x, zh))
    zn = (at(y, x, zh + 1), at(y, x, zh - 1))
    partner = {"rep": zl * 2 + 1 - core}
    line = [{"rep": ((zl + k) % 4) * 2 + core} for k in (1, 2, 3)]

    def mine(t, h):
        return (tok_hbm, cot_hbm)[t].at[:, pl.ds(256 * h, 256)]

    own = [
        pltpu.make_async_copy(mine(t, h), g.at[t, h, 0, 0, 0], own_sem.at[t, h])
        for t in (TOK, COT)
        for h in range(2)
    ]
    loads = [
        pltpu.make_async_copy(src, dst, load_sem.at[i])
        for i, (src, dst) in enumerate(
            ((delta_hbm, delta_v), (gate_hbm, gate_w), (up_hbm, up_w), (down_hbm, down_w), (gain_hbm, gain_ref))
        )
    ]
    for load in own:
        load.start()
    barrier = pltpu.get_barrier_semaphore()
    peers = [*zn, *line, partner, *xn, *yn]
    for peer in peers:
        pl.semaphore_signal(barrier, inc=1, device_id=peer, device_id_type=MESH)
    for load in own:
        load.wait()
    pl.semaphore_wait(barrier, len(peers))

    started, arrived = {}, set()

    def start(key, src, dst, ssem, rsem, device):
        copy = pltpu.make_async_remote_copy(
            src_ref=src, dst_ref=dst, send_sem=ssem, recv_sem=rsem,
            device_id=device, device_id_type=MESH,
        )
        copy.start()
        started[key] = copy

    def need(key):
        if key not in arrived:
            arrived.add(key)
            started[key].wait_recv()

    def xy(task, h, k, src, dst, device):
        t, rz = task
        start((task, h, k), src, dst, send.at[t, h, rz, k], recv.at[t, h, rz, k], device)

    def near(h):
        return (xn, yn) if h == 0 else (yn, xn)

    lo, hi = pl.ds(0, 32), pl.ds(32, 32)

    def first_send(task):
        for h in range(2):
            b = g.at[task[0], h, task[1]]
            src = b.at[0, 0]
            xy(task, h, 0, src, b.at[0, 3], near(h)[0][0])
            xy(task, h, 1, src, b.at[0, 1], near(h)[0][1])

    def first_forward(task):
        for h in range(2):
            b = g.at[task[0], h, task[1]]
            need((task, h, 0))
            xy(task, h, 2, b.at[0, 3, lo], b.at[0, 2, lo], near(h)[0][0])
            need((task, h, 1))
            xy(task, h, 3, b.at[0, 1, hi], b.at[0, 2, hi], near(h)[0][1])

    brings = {0: (), 1: (1,), 2: (2, 3), 3: (0,)}

    def second_send(task, i):
        first, last = GROUPS[task][i]
        for h in range(2):
            b = g.at[task[0], h, task[1]]
            for offset in range(first, last):
                for k in brings[offset]:
                    need((task, h, k))
            cols = pl.ds(first, last - first)
            src = b.at[0, cols]
            xy(task, h, 4 + 4 * i, src, b.at[3, cols], near(h)[1][0])
            xy(task, h, 5 + 4 * i, src, b.at[1, cols], near(h)[1][1])

    def second_forward(task, i):
        first, last = GROUPS[task][i]
        for h in range(2):
            b = g.at[task[0], h, task[1]]
            cols = pl.ds(first, last - first)
            need((task, h, 4 + 4 * i))
            xy(task, h, 6 + 4 * i, b.at[3, cols, lo], b.at[2, cols, lo], near(h)[1][0])
            need((task, h, 5 + 4 * i))
            xy(task, h, 7 + 4 * i, b.at[1, cols, hi], b.at[2, cols, hi], near(h)[1][1])

    def z_send(t):
        for h in range(2):
            start(("z", t, h, 0), g.at[t, h, 0, 0, 0], g.at[t, h, 3, 0, 0],
                  zsend.at[t, h, 0], zrecv.at[t, h, 0], zn[0])
        for h in (1, 0):
            start(("z", t, h, 1), g.at[t, h, 0, 0, 0], g.at[t, h, 1, 0, 0],
                  zsend.at[t, h, 1], zrecv.at[t, h, 1], zn[1])

    def z_forward(t):
        need(("z", t, 0, 0))
        start(("z", t, 0, 2), g.at[t, 0, 3, 0, 0], g.at[t, 0, 2, 0, 0],
              zsend.at[t, 0, 2], zrecv.at[t, 0, 2], zn[0])
        need(("z", t, 1, 1))
        start(("z", t, 1, 2), g.at[t, 1, 1, 0, 0], g.at[t, 1, 2, 0, 0],
              zsend.at[t, 1, 2], zrecv.at[t, 1, 2], zn[1])

    def z_need(task):
        t, rz = task
        if rz:
            for h in range(2):
                need(("z", t, h, {3: 0, 1: 1, 2: 2}[rz]))

    sent = set()

    def arrive(task):
        for h in range(2):
            for i in range(len(GROUPS[task])):
                need((task, h, 6 + 4 * i))
                need((task, h, 7 + 4 * i))
        for key, copy in started.items():
            if key[0] == task and key not in sent:
                sent.add(key)
                copy.wait_send()

    def outer_pack():
        loads[0].wait()

        @pl.loop(0, 8)
        def _(c):
            cols = pl.ds(pl.multiple_of(c * 512, 512), 512)
            rows = delta_v[:, cols].astype(F32)
            for b in range(8):
                if b < 7:
                    block = rows[b * 11 : b * 11 + 16]
                else:
                    block = jnp.concatenate([rows[77:88], jnp.zeros((5, 512), F32)], axis=0)
                share[b % 2, b // 2, :, cols] = block.astype(BF16)

    def outer_pair():
        start("pair", share.at[1 - core], pair_in, osend.at[0], orecv.at[0], partner)

    def outer_line():
        need("pair")

        @pl.loop(0, 4)
        def _(b):
            pair_out[b] = (share[core, b].astype(F32) + pair_in[b].astype(F32)).astype(BF16)

        for k in range(3):
            start(("line", k), pair_out.at[(zl + k + 1) % 4], line_in.at[k],
                  osend.at[1 + k], orecv.at[1 + k], line[k])

    def outer_finish():
        for k in range(3):
            need(("line", k))
        total = share[core, zl].astype(F32) + pair_in[zl].astype(F32)
        for k in range(3):
            total = total + line_in[k].astype(F32)
        total_out[...] = total

    def prep_gate_up():
        loads[1].wait()
        loads[2].wait()

        @pl.loop(0, 8)
        def _(c):
            cols = pl.ds(pl.multiple_of(c * 512, 512), 512)
            gate_up[:, cols] = jnp.concatenate(
                [gate_w[:, cols].astype(F32), up_w[:, cols].astype(F32)], axis=0
            ).astype(BF16)

    def prep_gain():
        loads[4].wait()

        rows = gain_ref[...].astype(F32)
        for c in range(32):
            gain_v[c * 128 : c * 128 + 128, :] = jnp.broadcast_to(rows[c : c + 1], (128, 128)).T

        acc_back[...] = jnp.zeros_like(acc_back)
        acc_pre[...] = jnp.zeros_like(acc_pre)
        squares[...] = jnp.zeros_like(squares)

    def prep_down():
        loads[3].wait()
        low = lax.broadcasted_iota(jnp.int32, (HID, 128), 1) < 64

        @pl.loop(0, 4)
        def _(yy):
            for pair in range(2):
                for xs in range(2):
                    a, b = (
                        down_w[
                            :, pl.ds(pl.multiple_of((yy * 4 + xx) * 256 + pair * 128, 128), 128)
                        ].astype(F32)
                        for xx in (2 * xs, 2 * xs + 1)
                    )
                    lanes = pl.ds(xs * 128, 128)
                    down_z[2 * pair, yy, :, lanes] = jnp.where(low, a, pltpu.roll(b, 64, 1)).astype(BF16)
                    down_z[2 * pair + 1, yy, :, lanes] = jnp.where(low, pltpu.roll(a, 64, 1), b).astype(BF16)

    def block_of(t, rz, ry, rx):
        return jnp.concatenate([g[t, 0, rz, ry, rx], g[t, 1, rz, rx, ry]], axis=1)

    def add_squares(task):
        arrive(task)

        @pl.loop(0, 16)
        def _(b):
            v = block_of(TOK, task[1], b // 4, b % 4).astype(F32)
            v = v * v
            part = v[:8]
            for i in range(1, 8):
                part = part + v[8 * i : 8 * i + 8]
            squares[...] += part

    def inverse_scale():
        total = jnp.sum(squares[...], axis=0, keepdims=True)
        squares[...] = jnp.broadcast_to(1.0 / jnp.sqrt(total / D + norm_epsilon), squares.shape)

    def forward(first, last):
        @pl.loop(first, last)
        def _(b):
            ry, rx = (b // 4 - y + 4) % 4, (b % 4 - x + 4) % 4
            cols = pl.ds(pl.multiple_of(b * 256, 256), 256)
            scale = squares[0:1, :]
            gain = gain_v[cols, :]
            gain = jnp.concatenate([gain] * 4, axis=1)
            raw = jnp.concatenate(
                [block_of(TOK, (zs - zh + 4) % 4, ry, rx) for zs in range(4)], axis=0
            )
            block = (raw.astype(F32) * scale * gain).astype(BF16)
            normed[cols, :] = block
            acc_pre[...] += lax.dot_general(
                gate_up[:, cols], block, NN, preferred_element_type=F32
            )

    def backward(task):
        arrive(task)
        rz = task[1]
        zs = (zh + rz) % 4

        @pl.loop(0, 4)
        def _(yy):
            ry = (yy - y + 4) % 4
            rows = jnp.concatenate(
                [block_of(COT, rz, ry, (xx - x + 4) % 4) for xx in range(4)], axis=0
            )
            acc_back[...] += lax.dot_general(
                down_z[zs, yy], rows, NN, preferred_element_type=F32
            )

    def finish():
        for q in range(4):
            lanes = pl.ds(q * 128, 128)
            gate_pre = acc_pre[:HID, lanes]
            up_pre = acc_pre[HID:, lanes]
            back = acc_back[:, lanes]
            sig = jax.nn.sigmoid(gate_pre)
            d_gate = back * up_pre * sig * (1.0 + gate_pre * (1.0 - sig))
            d_up = back * gate_pre * sig
            d_out[:, lanes] = jnp.concatenate([d_gate, d_up], axis=0).astype(BF16)

    def run(op):
        name, args = op[0], op[1:]
        task = args[:2]
        if name == "Z":
            z_send(args[0])
        elif name == "ZF":
            z_forward(args[0])
        elif name == "F":
            z_need(task)
            first_send(task)
        elif name == "FF":
            first_forward(task)
        elif name == "S":
            z_need(task)
            second_send(task, args[2])
        elif name == "SF":
            second_forward(task, args[2])
        elif name == "OP":
            outer_pack()
            outer_pair()
        elif name == "OL":
            outer_line()
        elif name == "OF":
            outer_finish()
        elif name == "PG":
            prep_gain()
        elif name == "PD":
            prep_down()
        elif name == "PU":
            prep_gate_up()
        elif name == "SQ":
            add_squares(task)
        elif name == "FW":
            if args[0] == 0:
                inverse_scale()
            forward(4 * args[0], 4 * args[0] + 4)
        elif name == "BW":
            backward(task)

    for i, op in enumerate(ORDER):
        if i == 3:
            for load in loads:
                load.start()
        run(op)
    finish()
    for key, copy in started.items():
        if key not in sent:
            copy.wait_send()


CHUNKS = 8


def finish_kernel(
    d_ref, normed_ref, total_ref, mom_ref, anchor_ref,
    grad_gate, grad_up, new_mom, new_anchor,
    gate_v, up_v, out_sem,
):
    wide = D // CHUNKS
    writes = []
    for c in range(CHUNKS):
        cols = pl.ds(c * wide, wide)
        out = lax.dot_general(d_ref[...], normed_ref[cols, :], NT, preferred_element_type=F32)
        gate_v[:, cols] = out[:HID].astype(BF16)
        up_v[:, cols] = out[HID:].astype(BF16)
        for i, (src, dst) in enumerate(((gate_v, grad_gate), (up_v, grad_up))):
            writes.append(
                pltpu.make_async_copy(src.at[:, cols], dst.at[:, cols], out_sem.at[c, i])
            )
            writes[-1].start()
    mean_delta = total_ref[:11] / 8.0
    momentum = outer_beta * mom_ref[...] + mean_delta
    new_mom[...] = momentum
    new_anchor[...] = (
        anchor_ref[...].astype(F32) - outer_rate * (mean_delta + outer_beta * momentum)
    ).astype(BF16)
    for write in writes:
        write.wait()


def body(
    tokens, norm_gain, gate_weight, up_weight, down_weight, cotangent, outer_delta, momentum, anchor
):
    vmem = pl.BlockSpec(memory_space=pltpu.VMEM)
    hbm = pl.BlockSpec(memory_space=pltpu.HBM)
    dma = pltpu.SemaphoreType.DMA
    d_t, normed, total = pl.pallas_call(
        kernel,
        out_shape=(
            pltpu.VMEM((2 * HID, 512), BF16),
            pltpu.VMEM((D, 512), BF16),
            pltpu.VMEM((16, D), F32),
        ),
        in_specs=[hbm] * 7,
        out_specs=(vmem, vmem, vmem),
        scratch_shapes=[
            pltpu.VMEM((2, 2, 4, 4, 4, 64, 256), BF16),
            pltpu.VMEM((HID, D), BF16),
            pltpu.VMEM((HID, D), BF16),
            pltpu.VMEM((HID, D), BF16),
            pltpu.VMEM((HID, D), BF16),
            pltpu.VMEM((2 * HID, D), BF16),
            pltpu.VMEM((4, 4, HID, 256), BF16),
            pltpu.VMEM((2 * HID, 512), F32),
            pltpu.VMEM((HID, 512), F32),
            pltpu.VMEM((8, 512), F32),
            pltpu.VMEM((D, 128), F32),
            pltpu.VMEM((32, 128), BF16),
            pltpu.VMEM((2, 4, 16, D), BF16),
            pltpu.VMEM((4, 16, D), BF16),
            pltpu.VMEM((4, 16, D), BF16),
            pltpu.VMEM((3, 16, D), BF16),
            dma((5,)),
            dma((2, 2)),
            dma((2, 2, 4, COPIES)),
            dma((2, 2, 4, COPIES)),
            dma((2, 2, 3)),
            dma((2, 2, 3)),
            dma((4,)),
            dma((4,)),
        ],
        compiler_params=pltpu.CompilerParams(
            collective_id=0, has_side_effects=True, vmem_limit_bytes=48 * 2**20
        ),
        cost_estimate=pl.CostEstimate(
            flops=6 * 512 * D * HID, bytes_accessed=8 * 2**20, transcendentals=512 * HID
        ),
        name="gather_and_forward",
    )(
        *(
            pltpu.with_memory_space_constraint(a, pltpu.HBM)
            for a in (
                tokens.T, cotangent.T, norm_gain.reshape(32, 128), gate_weight[0], up_weight[0], down_weight[0],
                outer_delta[0],
            )
        )
    )
    d_t, normed, total = (
        pltpu.with_memory_space_constraint(a, pltpu.VMEM) for a in (d_t, normed, total)
    )
    outs = pl.pallas_call(
        finish_kernel,
        out_shape=(
            jax.ShapeDtypeStruct((HID, D), BF16),
            jax.ShapeDtypeStruct((HID, D), BF16),
            jax.ShapeDtypeStruct((11, D), F32),
            jax.ShapeDtypeStruct((11, D), BF16),
        ),
        in_specs=[vmem, vmem, vmem, vmem, vmem],
        out_specs=(hbm, hbm, vmem, vmem),
        scratch_shapes=[
            pltpu.VMEM((HID, D), BF16),
            pltpu.VMEM((HID, D), BF16),
            dma((CHUNKS, 2)),
        ],
        compiler_params=pltpu.CompilerParams(vmem_limit_bytes=16 * 2**20),
        cost_estimate=pl.CostEstimate(
            flops=4 * 512 * D * HID, bytes_accessed=6 * 2**20, transcendentals=0
        ),
        name="gradients_and_outer_update",
    )(d_t, normed, total, momentum, anchor)
    return outs[0][None], outs[1][None], outs[2], outs[3]


def solution(mesh):
    return jax.shard_map(
        body,
        mesh=mesh,
        in_specs=(
            P("rep", "fsdp"),
            P(),
            P("rep", "fsdp", None),
            P("rep", "fsdp", None),
            P("rep", "fsdp", None),
            P("rep", "fsdp"),
            P("rep", "fsdp", None),
            P(("fsdp", "rep"), None),
            P(("fsdp", "rep"), None),
        ),
        out_specs=(
            P("rep", "fsdp", None),
            P("rep", "fsdp", None),
            P(("fsdp", "rep"), None),
            P(("fsdp", "rep"), None),
        ),
        check_vma=False,
    )
```

```python
import functools

import jax
import jax.numpy as jnp
from jax import lax
from jax.experimental import pallas as pl
from jax.experimental.pallas import tpu as pltpu
from jax.sharding import PartitionSpec as P

norm_epsilon = 1e-06
outer_beta = 0.9
outer_rate = 0.7

MESH = pl.DeviceIdType.MESH
F32 = jnp.float32
BF16 = jnp.bfloat16
D = 4096
HID = 88
NT = (((1,), (1,)), ((), ()))
NN = (((1,), (0,)), ((), ()))
TOK, COT = 0, 1
ORDER = (
    ('F', 0, 0), ('Z', 0), ('S', 0, 0, 0), ('F', 1, 0), ('S', 1, 0, 0), ('FF', 0, 0), ('SF', 0, 0, 0),
    ('FF', 1, 0), ('PG',), ('SF', 1, 0, 0), ('Z', 1), ('S', 0, 0, 1), ('S', 1, 0, 1), ('F', 0, 1),
    ('F', 0, 3), ('ZF', 0), ('S', 0, 1, 0), ('SF', 0, 0, 1), ('OP',), ('SF', 1, 0, 1), ('FF', 0, 1),
    ('S', 0, 3, 0), ('FF', 0, 3), ('ZF', 1), ('SF', 0, 1, 0), ('S', 1, 3, 0), ('F', 1, 3), ('F', 1, 1),
    ('S', 0, 1, 1), ('PD',), ('OL',), ('SQ', 0, 0), ('F', 0, 2), ('S', 0, 2, 0), ('S', 0, 3, 1),
    ('SF', 0, 1, 1), ('FF', 0, 2), ('F', 1, 2), ('S', 1, 1, 0), ('S', 1, 2, 0), ('SF', 0, 3, 0), ('FF', 1, 1),
    ('SF', 0, 2, 0), ('FF', 1, 3), ('S', 0, 2, 1), ('FF', 1, 2), ('SF', 0, 3, 1), ('BW', 1, 0), ('PU',),
    ('S', 1, 1, 1), ('SF', 0, 2, 1), ('S', 1, 3, 1), ('S', 1, 2, 1), ('SF', 1, 1, 0), ('SF', 1, 1, 1),
    ('SQ', 0, 3), ('SQ', 0, 1), ('SQ', 0, 2), ('SF', 1, 2, 0), ('FW', 0), ('SF', 1, 3, 0), ('OF',),
    ('SF', 1, 3, 1), ('FW', 1), ('SF', 1, 2, 1), ('FW', 2), ('FW', 3), ('BW', 1, 1), ('BW', 1, 3),
    ('BW', 1, 2),
)
GROUPS = {
    (0, 0): ((0, 1), (1, 4)),
    (1, 0): ((0, 1), (1, 4)),
    (0, 3): ((0, 1), (1, 4)),
    (0, 1): ((0, 1), (1, 4)),
    (1, 3): ((0, 1), (1, 4)),
    (0, 2): ((0, 1), (1, 4)),
    (1, 1): ((0, 1), (1, 4)),
    (1, 2): ((0, 1), (1, 4)),
}
COPIES = 4 + 4 * max(len(groups) for groups in GROUPS.values())


def kernel(
    tok_hbm, cot_hbm, gain_hbm, gate_hbm, up_hbm, down_hbm, delta_hbm,
    d_out, normed, total_out,
    g, gate_w, up_w, down_w, delta_v, gate_up, down_z, acc_pre, acc_back, squares, gain_v, gain_ref,
    share, pair_in, pair_out, line_in,
    load_sem, own_sem, send, recv, zsend, zrecv, osend, orecv,
):
    f = lax.axis_index("fsdp")
    r = lax.axis_index("rep")
    y, x, zh = f // 16, (f // 4) % 4, f % 4
    zl, core = r // 2, r % 2

    def at(yy, xx, zz):
        return {"fsdp": ((yy + 4) % 4) * 16 + ((xx + 4) % 4) * 4 + (zz + 4) % 4}

    xn = (at(y, x + 1, zh), at(y, x - 1, zh))
    yn = (at(y + 1, x, zh), at(y - 1, x, zh))
    zn = (at(y, x, zh + 1), at(y, x, zh - 1))
    partner = {"rep": zl * 2 + 1 - core}
    line = [{"rep": ((zl + k) % 4) * 2 + core} for k in (1, 2, 3)]

    def mine(t, h):
        return (tok_hbm, cot_hbm)[t].at[:, pl.ds(256 * h, 256)]

    own = [
        pltpu.make_async_copy(mine(t, h), g.at[t, h, 0, 0, 0], own_sem.at[t, h])
        for t in (TOK, COT)
        for h in range(2)
    ]
    loads = [
        pltpu.make_async_copy(src, dst, load_sem.at[i])
        for i, (src, dst) in enumerate(
            ((delta_hbm, delta_v), (gate_hbm, gate_w), (up_hbm, up_w), (down_hbm, down_w), (gain_hbm, gain_ref))
        )
    ]
    barrier = pltpu.get_barrier_semaphore()
    peers = [*xn, *yn, *zn, *line, partner]
    for i, peer in enumerate(peers):
        pl.semaphore_signal(barrier, inc=1, device_id=peer, device_id_type=MESH)
        if i == 5:
            for load in own:
                load.start()
    for load in own:
        load.wait()
    pl.semaphore_wait(barrier, len(peers))

    started, arrived = {}, set()

    def start(key, src, dst, ssem, rsem, device):
        copy = pltpu.make_async_remote_copy(
            src_ref=src, dst_ref=dst, send_sem=ssem, recv_sem=rsem,
            device_id=device, device_id_type=MESH,
        )
        copy.start()
        started[key] = copy

    def need(key):
        if key not in arrived:
            arrived.add(key)
            started[key].wait_recv()

    def xy(task, h, k, src, dst, device):
        t, rz = task
        start((task, h, k), src, dst, send.at[t, h, rz, k], recv.at[t, h, rz, k], device)

    def near(h):
        return (xn, yn) if h == 0 else (yn, xn)

    lo, hi = pl.ds(0, 32), pl.ds(32, 32)

    def first_send(task):
        for h in range(2):
            b = g.at[task[0], h, task[1]]
            src = b.at[0, 0]
            xy(task, h, 0, src, b.at[0, 3], near(h)[0][0])
            xy(task, h, 1, src, b.at[0, 1], near(h)[0][1])

    def first_forward(task):
        for h in range(2):
            b = g.at[task[0], h, task[1]]
            need((task, h, 0))
            xy(task, h, 2, b.at[0, 3, lo], b.at[0, 2, lo], near(h)[0][0])
            need((task, h, 1))
            xy(task, h, 3, b.at[0, 1, hi], b.at[0, 2, hi], near(h)[0][1])

    brings = {0: (), 1: (1,), 2: (2, 3), 3: (0,)}

    def second_send(task, i):
        first, last = GROUPS[task][i]
        for h in range(2):
            b = g.at[task[0], h, task[1]]
            for offset in range(first, last):
                for k in brings[offset]:
                    need((task, h, k))
            cols = pl.ds(first, last - first)
            src = b.at[0, cols]
            xy(task, h, 4 + 4 * i, src, b.at[3, cols], near(h)[1][0])
            xy(task, h, 5 + 4 * i, src, b.at[1, cols], near(h)[1][1])

    def second_forward(task, i):
        first, last = GROUPS[task][i]
        for h in range(2):
            b = g.at[task[0], h, task[1]]
            cols = pl.ds(first, last - first)
            need((task, h, 4 + 4 * i))
            xy(task, h, 6 + 4 * i, b.at[3, cols, lo], b.at[2, cols, lo], near(h)[1][0])
            need((task, h, 5 + 4 * i))
            xy(task, h, 7 + 4 * i, b.at[1, cols, hi], b.at[2, cols, hi], near(h)[1][1])

    def z_send(t):
        for h in range(2):
            start(("z", t, h, 0), g.at[t, h, 0, 0, 0], g.at[t, h, 3, 0, 0],
                  zsend.at[t, h, 0], zrecv.at[t, h, 0], zn[0])
        for h in (1, 0):
            start(("z", t, h, 1), g.at[t, h, 0, 0, 0], g.at[t, h, 1, 0, 0],
                  zsend.at[t, h, 1], zrecv.at[t, h, 1], zn[1])

    def z_forward(t):
        need(("z", t, 0, 0))
        start(("z", t, 0, 2), g.at[t, 0, 3, 0, 0], g.at[t, 0, 2, 0, 0],
              zsend.at[t, 0, 2], zrecv.at[t, 0, 2], zn[0])
        need(("z", t, 1, 1))
        start(("z", t, 1, 2), g.at[t, 1, 1, 0, 0], g.at[t, 1, 2, 0, 0],
              zsend.at[t, 1, 2], zrecv.at[t, 1, 2], zn[1])

    def z_need(task):
        t, rz = task
        if rz:
            for h in range(2):
                need(("z", t, h, {3: 0, 1: 1, 2: 2}[rz]))

    sent = set()

    def arrive(task):
        for h in range(2):
            for i in range(len(GROUPS[task])):
                need((task, h, 6 + 4 * i))
                need((task, h, 7 + 4 * i))
        for key, copy in started.items():
            if key[0] == task and key not in sent:
                sent.add(key)
                copy.wait_send()

    def outer_pack():
        loads[0].wait()

        @pl.loop(0, 8)
        def _(c):
            cols = pl.ds(pl.multiple_of(c * 512, 512), 512)
            rows = delta_v[:, cols].astype(F32)
            for b in range(8):
                if b < 7:
                    block = rows[b * 11 : b * 11 + 16]
                else:
                    block = jnp.concatenate([rows[77:88], jnp.zeros((5, 512), F32)], axis=0)
                share[b % 2, b // 2, :, cols] = block.astype(BF16)

    def outer_pair():
        start("pair", share.at[1 - core], pair_in, osend.at[0], orecv.at[0], partner)

    def outer_line():
        need("pair")

        @pl.loop(0, 4)
        def _(b):
            pair_out[b] = (share[core, b].astype(F32) + pair_in[b].astype(F32)).astype(BF16)

        for k in range(3):
            start(("line", k), pair_out.at[(zl + k + 1) % 4], line_in.at[k],
                  osend.at[1 + k], orecv.at[1 + k], line[k])

    def outer_finish():
        for k in range(3):
            need(("line", k))
        total = share[core, zl].astype(F32) + pair_in[zl].astype(F32)
        for k in range(3):
            total = total + line_in[k].astype(F32)
        total_out[...] = total

    def prep_gate_up():
        loads[1].wait()
        loads[2].wait()

        @pl.loop(0, 8)
        def _(c):
            cols = pl.ds(pl.multiple_of(c * 512, 512), 512)
            gate_up[:, cols] = jnp.concatenate(
                [gate_w[:, cols].astype(F32), up_w[:, cols].astype(F32)], axis=0
            ).astype(BF16)

    def prep_gain():
        loads[4].wait()

        rows = gain_ref[...].astype(F32)
        for c in range(32):
            gain_v[c * 128 : c * 128 + 128, :] = jnp.broadcast_to(rows[c : c + 1], (128, 128)).T

        acc_back[...] = jnp.zeros_like(acc_back)
        acc_pre[...] = jnp.zeros_like(acc_pre)
        squares[...] = jnp.zeros_like(squares)

    def prep_down():
        loads[3].wait()
        low = lax.broadcasted_iota(jnp.int32, (HID, 128), 1) < 64

        @pl.loop(0, 4)
        def _(yy):
            for pair in range(2):
                for xs in range(2):
                    a, b = (
                        down_w[
                            :, pl.ds(pl.multiple_of((yy * 4 + xx) * 256 + pair * 128, 128), 128)
                        ].astype(F32)
                        for xx in (2 * xs, 2 * xs + 1)
                    )
                    lanes = pl.ds(xs * 128, 128)
                    down_z[2 * pair, yy, :, lanes] = jnp.where(low, a, pltpu.roll(b, 64, 1)).astype(BF16)
                    down_z[2 * pair + 1, yy, :, lanes] = jnp.where(low, pltpu.roll(a, 64, 1), b).astype(BF16)

    def block_of(t, rz, ry, rx):
        return jnp.concatenate([g[t, 0, rz, ry, rx], g[t, 1, rz, rx, ry]], axis=1)

    def add_squares(task):
        arrive(task)

        @pl.loop(0, 16)
        def _(b):
            v = block_of(TOK, task[1], b // 4, b % 4).astype(F32)
            v = v * v
            part = v[:8]
            for i in range(1, 8):
                part = part + v[8 * i : 8 * i + 8]
            squares[...] += part

    def inverse_scale():
        total = jnp.sum(squares[...], axis=0, keepdims=True)
        squares[...] = jnp.broadcast_to(1.0 / jnp.sqrt(total / D + norm_epsilon), squares.shape)

    def forward(first, last):
        @pl.loop(first, last)
        def _(b):
            ry, rx = (b // 4 - y + 4) % 4, (b % 4 - x + 4) % 4
            cols = pl.ds(pl.multiple_of(b * 256, 256), 256)
            scale = squares[0:1, :]
            gain = gain_v[cols, :]
            gain = jnp.concatenate([gain] * 4, axis=1)
            raw = jnp.concatenate(
                [block_of(TOK, (zs - zh + 4) % 4, ry, rx) for zs in range(4)], axis=0
            )
            block = (raw.astype(F32) * scale * gain).astype(BF16)
            normed[:, cols] = block.T
            acc_pre[...] += lax.dot_general(
                gate_up[:, cols], block, NN, preferred_element_type=F32
            )

    def backward(task):
        arrive(task)
        rz = task[1]
        zs = (zh + rz) % 4

        @pl.loop(0, 4)
        def _(yy):
            ry = (yy - y + 4) % 4
            rows = jnp.concatenate(
                [block_of(COT, rz, ry, (xx - x + 4) % 4) for xx in range(4)], axis=0
            )
            acc_back[...] += lax.dot_general(
                down_z[zs, yy], rows, NN, preferred_element_type=F32
            )

    def finish():
        for q in range(4):
            lanes = pl.ds(q * 128, 128)
            gate_pre = acc_pre[:HID, lanes]
            up_pre = acc_pre[HID:, lanes]
            back = acc_back[:, lanes]
            sig = jax.nn.sigmoid(gate_pre)
            d_gate = back * up_pre * sig * (1.0 + gate_pre * (1.0 - sig))
            d_up = back * gate_pre * sig
            d_out[:, lanes] = jnp.concatenate([d_gate, d_up], axis=0).astype(BF16)

    def run(op):
        name, args = op[0], op[1:]
        task = args[:2]
        if name == "Z":
            z_send(args[0])
        elif name == "ZF":
            z_forward(args[0])
        elif name == "F":
            z_need(task)
            first_send(task)
        elif name == "FF":
            first_forward(task)
        elif name == "S":
            z_need(task)
            second_send(task, args[2])
        elif name == "SF":
            second_forward(task, args[2])
        elif name == "OP":
            outer_pack()
            outer_pair()
        elif name == "OL":
            outer_line()
        elif name == "OF":
            outer_finish()
        elif name == "PG":
            prep_gain()
        elif name == "PD":
            prep_down()
        elif name == "PU":
            prep_gate_up()
        elif name == "SQ":
            add_squares(task)
        elif name == "FW":
            if args[0] == 0:
                inverse_scale()
            forward(4 * args[0], 4 * args[0] + 4)
        elif name == "BW":
            backward(task)

    for i, op in enumerate(ORDER):
        if i == 3:
            for load in loads:
                load.start()
        run(op)
    finish()
    for key, copy in started.items():
        if key not in sent:
            copy.wait_send()


CHUNKS = 8


def finish_kernel(
    d_ref, normed_ref, total_ref, mom_ref, anchor_ref,
    grad_gate, grad_up, new_mom, new_anchor,
    gate_v, up_v, out_sem,
):
    wide = D // CHUNKS
    writes = []
    for c in range(CHUNKS):
        cols = pl.ds(c * wide, wide)
        out = lax.dot_general(d_ref[...], normed_ref[:, cols], NN, preferred_element_type=F32)
        gate_v[:, cols] = out[:HID].astype(BF16)
        up_v[:, cols] = out[HID:].astype(BF16)
        for i, (src, dst) in enumerate(((gate_v, grad_gate), (up_v, grad_up))):
            writes.append(
                pltpu.make_async_copy(src.at[:, cols], dst.at[:, cols], out_sem.at[c, i])
            )
            writes[-1].start()
    mean_delta = total_ref[:11] / 8.0
    momentum = outer_beta * mom_ref[...] + mean_delta
    new_mom[...] = momentum
    new_anchor[...] = (
        anchor_ref[...].astype(F32) - outer_rate * (mean_delta + outer_beta * momentum)
    ).astype(BF16)
    for write in writes:
        write.wait()


def body(
    tokens, norm_gain, gate_weight, up_weight, down_weight, cotangent, outer_delta, momentum, anchor
):
    vmem = pl.BlockSpec(memory_space=pltpu.VMEM)
    hbm = pl.BlockSpec(memory_space=pltpu.HBM)
    dma = pltpu.SemaphoreType.DMA
    d_t, normed, total = pl.pallas_call(
        kernel,
        out_shape=(
            pltpu.VMEM((2 * HID, 512), BF16),
            pltpu.VMEM((512, D), BF16),
            pltpu.VMEM((16, D), F32),
        ),
        in_specs=[hbm] * 7,
        out_specs=(vmem, vmem, vmem),
        scratch_shapes=[
            pltpu.VMEM((2, 2, 4, 4, 4, 64, 256), BF16),
            pltpu.VMEM((HID, D), BF16),
            pltpu.VMEM((HID, D), BF16),
            pltpu.VMEM((HID, D), BF16),
            pltpu.VMEM((HID, D), BF16),
            pltpu.VMEM((2 * HID, D), BF16),
            pltpu.VMEM((4, 4, HID, 256), BF16),
            pltpu.VMEM((2 * HID, 512), F32),
            pltpu.VMEM((HID, 512), F32),
            pltpu.VMEM((8, 512), F32),
            pltpu.VMEM((D, 128), F32),
            pltpu.VMEM((32, 128), BF16),
            pltpu.VMEM((2, 4, 16, D), BF16),
            pltpu.VMEM((4, 16, D), BF16),
            pltpu.VMEM((4, 16, D), BF16),
            pltpu.VMEM((3, 16, D), BF16),
            dma((5,)),
            dma((2, 2)),
            dma((2, 2, 4, COPIES)),
            dma((2, 2, 4, COPIES)),
            dma((2, 2, 3)),
            dma((2, 2, 3)),
            dma((4,)),
            dma((4,)),
        ],
        compiler_params=pltpu.CompilerParams(
            collective_id=0, has_side_effects=True, vmem_limit_bytes=48 * 2**20
        ),
        cost_estimate=pl.CostEstimate(
            flops=6 * 512 * D * HID, bytes_accessed=8 * 2**20, transcendentals=512 * HID
        ),
        name="gather_and_forward",
    )(
        *(
            pltpu.with_memory_space_constraint(a, pltpu.HBM)
            for a in (
                tokens.T, cotangent.T, norm_gain.reshape(32, 128), gate_weight[0], up_weight[0], down_weight[0],
                outer_delta[0],
            )
        )
    )
    d_t, normed, total = (
        pltpu.with_memory_space_constraint(a, pltpu.VMEM) for a in (d_t, normed, total)
    )
    outs = pl.pallas_call(
        finish_kernel,
        out_shape=(
            jax.ShapeDtypeStruct((HID, D), BF16),
            jax.ShapeDtypeStruct((HID, D), BF16),
            jax.ShapeDtypeStruct((11, D), F32),
            jax.ShapeDtypeStruct((11, D), BF16),
        ),
        in_specs=[vmem, vmem, vmem, vmem, vmem],
        out_specs=(hbm, hbm, vmem, vmem),
        scratch_shapes=[
            pltpu.VMEM((HID, D), BF16),
            pltpu.VMEM((HID, D), BF16),
            dma((CHUNKS, 2)),
        ],
        compiler_params=pltpu.CompilerParams(vmem_limit_bytes=16 * 2**20),
        cost_estimate=pl.CostEstimate(
            flops=4 * 512 * D * HID, bytes_accessed=6 * 2**20, transcendentals=0
        ),
        name="gradients_and_outer_update",
    )(d_t, normed, total, momentum, anchor)
    return outs[0][None], outs[1][None], outs[2], outs[3]


def solution(mesh):
    return jax.shard_map(
        body,
        mesh=mesh,
        in_specs=(
            P("rep", "fsdp"),
            P(),
            P("rep", "fsdp", None),
            P("rep", "fsdp", None),
            P("rep", "fsdp", None),
            P("rep", "fsdp"),
            P("rep", "fsdp", None),
            P(("fsdp", "rep"), None),
            P(("fsdp", "rep"), None),
        ),
        out_specs=(
            P("rep", "fsdp", None),
            P("rep", "fsdp", None),
            P(("fsdp", "rep"), None),
            P(("fsdp", "rep"), None),
        ),
        check_vma=False,
    )
```

```python
import functools

import jax
import jax.numpy as jnp
from jax import lax
from jax.experimental import pallas as pl
from jax.experimental.pallas import tpu as pltpu
from jax.sharding import PartitionSpec as P

norm_epsilon = 1e-06
outer_beta = 0.9
outer_rate = 0.7

MESH = pl.DeviceIdType.MESH
F32 = jnp.float32
BF16 = jnp.bfloat16
D = 4096
HID = 88
NT = (((1,), (1,)), ((), ()))
NN = (((1,), (0,)), ((), ()))
TOK, COT = 0, 1
DIRECT = ((TOK, 0), (COT, 0))
ORDER = (
    ('Z', 0), ('F', 0, 0), ('Z', 1), ('F', 1, 0), ('S', 0, 0, 0), ('S', 1, 0, 0), ('PG',), ('OP',),
    ('S', 0, 0, 1), ('PU',), ('S', 1, 0, 1), ('SF', 1, 0, 0), ('SF', 0, 0, 0), ('ZF', 0), ('S', 0, 1, 0),
    ('F', 0, 1), ('F', 0, 3), ('S', 0, 3, 0), ('SF', 1, 0, 1), ('SF', 0, 0, 1), ('FF', 0, 1), ('SF', 0, 1, 0),
    ('FF', 0, 3), ('SF', 0, 3, 0), ('S', 1, 3, 0), ('ZF', 1), ('F', 1, 3), ('F', 1, 1), ('S', 0, 1, 1),
    ('F', 0, 2), ('S', 1, 1, 0), ('S', 0, 3, 1), ('PD',), ('SQ', 0, 0), ('OL',), ('FF', 1, 3), ('FF', 1, 1),
    ('FF', 0, 2), ('S', 0, 2, 0), ('F', 1, 2), ('SF', 0, 1, 1), ('SF', 0, 3, 1), ('BW', 1, 0), ('S', 0, 2, 1),
    ('SF', 0, 2, 0), ('FF', 1, 2), ('S', 1, 2, 0), ('S', 1, 3, 1), ('SF', 0, 2, 1), ('S', 1, 1, 1),
    ('S', 1, 2, 1), ('SQ', 0, 3), ('SF', 1, 3, 1), ('SQ', 0, 2), ('SQ', 0, 1), ('SF', 1, 3, 0),
    ('SF', 1, 1, 0), ('SF', 1, 2, 0), ('FW', 0), ('SF', 1, 1, 1), ('FW', 1), ('SF', 1, 2, 1), ('OF',),
    ('FW', 2), ('FW', 3), ('BW', 1, 3), ('BW', 1, 1), ('BW', 1, 2),
)
GROUPS = {
    (0, 0): ((0, 1), (1, 4)),
    (1, 0): ((0, 1), (1, 4)),
    (0, 3): ((0, 1), (1, 4)),
    (0, 1): ((0, 1), (1, 4)),
    (1, 3): ((0, 1), (1, 4)),
    (0, 2): ((0, 1), (1, 4)),
    (1, 1): ((0, 1), (1, 4)),
    (1, 2): ((0, 1), (1, 4)),
}
COPIES = 4 + 4 * max(len(groups) for groups in GROUPS.values())


def kernel(
    tok_hbm, cot_hbm, gain_hbm, gate_hbm, up_hbm, down_hbm, delta_hbm,
    d_out, normed, total_out,
    g, gate_w, up_w, down_w, delta_v, gate_up, down_z, acc_pre, acc_back, squares, gain_v, gain_ref,
    share, pair_in, pair_out, line_in,
    load_sem, own_sem, send, recv, zsend, zrecv, osend, orecv,
):
    f = lax.axis_index("fsdp")
    r = lax.axis_index("rep")
    y, x, zh = f // 16, (f // 4) % 4, f % 4
    zl, core = r // 2, r % 2

    def at(yy, xx, zz):
        return {"fsdp": ((yy + 4) % 4) * 16 + ((xx + 4) % 4) * 4 + (zz + 4) % 4}

    xn = (at(y, x + 1, zh), at(y, x - 1, zh), at(y, x + 2, zh))
    yn = (at(y + 1, x, zh), at(y - 1, x, zh), at(y + 2, x, zh))
    zn = (at(y, x, zh + 1), at(y, x, zh - 1))
    partner = {"rep": zl * 2 + 1 - core}
    line = [{"rep": ((zl + k) % 4) * 2 + core} for k in (1, 2, 3)]

    def mine(t, h):
        return (tok_hbm, cot_hbm)[t].at[:, pl.ds(256 * h, 256)]

    own = [
        pltpu.make_async_copy(mine(t, h), g.at[t, h, 0, 0, 0], own_sem.at[t, h])
        for t in (TOK, COT)
        for h in range(2)
    ]
    loads = [
        pltpu.make_async_copy(src, dst, load_sem.at[i])
        for i, (src, dst) in enumerate(
            ((delta_hbm, delta_v), (gate_hbm, gate_w), (up_hbm, up_w), (down_hbm, down_w), (gain_hbm, gain_ref))
        )
    ]
    barrier = pltpu.get_barrier_semaphore()
    peers = [*xn, *yn, *zn, *line, partner]
    for i, peer in enumerate(peers):
        pl.semaphore_signal(barrier, inc=1, device_id=peer, device_id_type=MESH)
        if i == 5:
            for load in own:
                load.start()
    for load in own:
        load.wait()
    pl.semaphore_wait(barrier, len(peers))

    started, arrived = {}, set()

    def start(key, src, dst, ssem, rsem, device):
        copy = pltpu.make_async_remote_copy(
            src_ref=src, dst_ref=dst, send_sem=ssem, recv_sem=rsem,
            device_id=device, device_id_type=MESH,
        )
        copy.start()
        started[key] = copy

    def need(key):
        if key not in arrived:
            arrived.add(key)
            started[key].wait_recv()

    def xy(task, h, k, src, dst, device):
        t, rz = task
        start((task, h, k), src, dst, send.at[t, h, rz, k], recv.at[t, h, rz, k], device)

    def near(h):
        return (xn, yn) if h == 0 else (yn, xn)

    lo, hi = pl.ds(0, 32), pl.ds(32, 32)

    def first_send(task):
        for h in range(2):
            b = g.at[task[0], h, task[1]]
            src = b.at[0, 0]
            xy(task, h, 0, src, b.at[0, 3], near(h)[0][0])
            xy(task, h, 1, src, b.at[0, 1], near(h)[0][1])
            if task in DIRECT:
                xy(task, h, 2, src, b.at[0, 2], near(h)[0][2])

    def first_forward(task):
        if task in DIRECT:
            return
        for h in range(2):
            b = g.at[task[0], h, task[1]]
            need((task, h, 0))
            xy(task, h, 2, b.at[0, 3, lo], b.at[0, 2, lo], near(h)[0][0])
            need((task, h, 1))
            xy(task, h, 3, b.at[0, 1, hi], b.at[0, 2, hi], near(h)[0][1])

    brings = {0: (), 1: (1,), 2: (2, 3), 3: (0,)}

    def second_send(task, i):
        first, last = GROUPS[task][i]
        for h in range(2):
            b = g.at[task[0], h, task[1]]
            for offset in range(first, last):
                for k in (2,) if task in DIRECT and offset == 2 else brings[offset]:
                    need((task, h, k))
            cols = pl.ds(first, last - first)
            src = b.at[0, cols]
            xy(task, h, 4 + 4 * i, src, b.at[3, cols], near(h)[1][0])
            xy(task, h, 5 + 4 * i, src, b.at[1, cols], near(h)[1][1])

    def second_forward(task, i):
        first, last = GROUPS[task][i]
        for h in range(2):
            b = g.at[task[0], h, task[1]]
            cols = pl.ds(first, last - first)
            need((task, h, 4 + 4 * i))
            xy(task, h, 6 + 4 * i, b.at[3, cols, lo], b.at[2, cols, lo], near(h)[1][0])
            need((task, h, 5 + 4 * i))
            xy(task, h, 7 + 4 * i, b.at[1, cols, hi], b.at[2, cols, hi], near(h)[1][1])

    def z_send(t):
        for h in range(2):
            start(("z", t, h, 0), g.at[t, h, 0, 0, 0], g.at[t, h, 3, 0, 0],
                  zsend.at[t, h, 0], zrecv.at[t, h, 0], zn[0])
        for h in (1, 0):
            start(("z", t, h, 1), g.at[t, h, 0, 0, 0], g.at[t, h, 1, 0, 0],
                  zsend.at[t, h, 1], zrecv.at[t, h, 1], zn[1])

    def z_forward(t):
        need(("z", t, 0, 0))
        start(("z", t, 0, 2), g.at[t, 0, 3, 0, 0], g.at[t, 0, 2, 0, 0],
              zsend.at[t, 0, 2], zrecv.at[t, 0, 2], zn[0])
        need(("z", t, 1, 1))
        start(("z", t, 1, 2), g.at[t, 1, 1, 0, 0], g.at[t, 1, 2, 0, 0],
              zsend.at[t, 1, 2], zrecv.at[t, 1, 2], zn[1])

    def z_need(task):
        t, rz = task
        if rz:
            for h in range(2):
                need(("z", t, h, {3: 0, 1: 1, 2: 2}[rz]))

    sent = set()

    def arrive(task):
        for h in range(2):
            for i in range(len(GROUPS[task])):
                need((task, h, 6 + 4 * i))
                need((task, h, 7 + 4 * i))
        for key, copy in started.items():
            if key[0] == task and key not in sent:
                sent.add(key)
                copy.wait_send()

    def outer_pack():
        loads[0].wait()

        @pl.loop(0, 8)
        def _(c):
            cols = pl.ds(pl.multiple_of(c * 512, 512), 512)
            rows = delta_v[:, cols].astype(F32)
            for b in range(8):
                if b < 7:
                    block = rows[b * 11 : b * 11 + 16]
                else:
                    block = jnp.concatenate([rows[77:88], jnp.zeros((5, 512), F32)], axis=0)
                share[b % 2, b // 2, :, cols] = block.astype(BF16)

    def outer_pair():
        start("pair", share.at[1 - core], pair_in, osend.at[0], orecv.at[0], partner)

    def outer_line():
        need("pair")

        @pl.loop(0, 4)
        def _(b):
            pair_out[b] = (share[core, b].astype(F32) + pair_in[b].astype(F32)).astype(BF16)

        for k in range(3):
            start(("line", k), pair_out.at[(zl + k + 1) % 4], line_in.at[k],
                  osend.at[1 + k], orecv.at[1 + k], line[k])

    def outer_finish():
        for k in range(3):
            need(("line", k))
        total = share[core, zl].astype(F32) + pair_in[zl].astype(F32)
        for k in range(3):
            total = total + line_in[k].astype(F32)
        total_out[...] = total

    def prep_gate_up():
        loads[1].wait()
        loads[2].wait()

        @pl.loop(0, 8)
        def _(c):
            cols = pl.ds(pl.multiple_of(c * 512, 512), 512)
            gate_up[:, cols] = jnp.concatenate(
                [gate_w[:, cols].astype(F32), up_w[:, cols].astype(F32)], axis=0
            ).astype(BF16)

    def prep_gain():
        loads[4].wait()

        rows = gain_ref[...].astype(F32)
        for c in range(32):
            gain_v[c * 128 : c * 128 + 128, :] = jnp.broadcast_to(rows[c : c + 1], (128, 128)).T

        acc_back[...] = jnp.zeros_like(acc_back)
        acc_pre[...] = jnp.zeros_like(acc_pre)
        squares[...] = jnp.zeros_like(squares)

    def prep_down():
        loads[3].wait()
        low = lax.broadcasted_iota(jnp.int32, (HID, 128), 1) < 64

        @pl.loop(0, 4)
        def _(yy):
            for pair in range(2):
                for xs in range(2):
                    a, b = (
                        down_w[
                            :, pl.ds(pl.multiple_of((yy * 4 + xx) * 256 + pair * 128, 128), 128)
                        ].astype(F32)
                        for xx in (2 * xs, 2 * xs + 1)
                    )
                    lanes = pl.ds(xs * 128, 128)
                    down_z[2 * pair, yy, :, lanes] = jnp.where(low, a, pltpu.roll(b, 64, 1)).astype(BF16)
                    down_z[2 * pair + 1, yy, :, lanes] = jnp.where(low, pltpu.roll(a, 64, 1), b).astype(BF16)

    def block_of(t, rz, ry, rx):
        return jnp.concatenate([g[t, 0, rz, ry, rx], g[t, 1, rz, rx, ry]], axis=1)

    def add_squares(task):
        arrive(task)

        @pl.loop(0, 16)
        def _(b):
            v = block_of(TOK, task[1], b // 4, b % 4).astype(F32)
            v = v * v
            part = v[:8]
            for i in range(1, 8):
                part = part + v[8 * i : 8 * i + 8]
            squares[...] += part

    def inverse_scale():
        total = jnp.sum(squares[...], axis=0, keepdims=True)
        squares[...] = jnp.broadcast_to(1.0 / jnp.sqrt(total / D + norm_epsilon), squares.shape)

    def forward(first, last):
        @pl.loop(first, last, unroll=2)
        def _(b):
            ry, rx = (b // 4 - y + 4) % 4, (b % 4 - x + 4) % 4
            cols = pl.ds(pl.multiple_of(b * 256, 256), 256)
            scale = squares[0:1, :]
            gain = gain_v[cols, :]
            gain = jnp.concatenate([gain] * 4, axis=1)
            raw = jnp.concatenate(
                [block_of(TOK, (zs - zh + 4) % 4, ry, rx) for zs in range(4)], axis=0
            )
            block = (raw.astype(F32) * scale * gain).astype(BF16)
            normed[:, cols] = block.T
            acc_pre[...] += lax.dot_general(
                gate_up[:, cols], block, NN, preferred_element_type=F32
            )

    def backward(task):
        arrive(task)
        rz = task[1]
        zs = (zh + rz) % 4

        @pl.loop(0, 4, unroll=4)
        def _(yy):
            ry = (yy - y + 4) % 4
            rows = jnp.concatenate(
                [block_of(COT, rz, ry, (xx - x + 4) % 4) for xx in range(4)], axis=0
            )
            acc_back[...] += lax.dot_general(
                down_z[zs, yy], rows, NN, preferred_element_type=F32
            )

    def finish():
        for q in range(4):
            lanes = pl.ds(q * 128, 128)
            gate_pre = acc_pre[:HID, lanes]
            up_pre = acc_pre[HID:, lanes]
            back = acc_back[:, lanes]
            sig = jax.nn.sigmoid(gate_pre)
            d_gate = back * up_pre * sig * (1.0 + gate_pre * (1.0 - sig))
            d_up = back * gate_pre * sig
            d_out[:, lanes] = jnp.concatenate([d_gate, d_up], axis=0).astype(BF16)

    def run(op):
        name, args = op[0], op[1:]
        task = args[:2]
        if name == "Z":
            z_send(args[0])
        elif name == "ZF":
            z_forward(args[0])
        elif name == "F":
            z_need(task)
            first_send(task)
        elif name == "FF":
            first_forward(task)
        elif name == "S":
            z_need(task)
            second_send(task, args[2])
        elif name == "SF":
            second_forward(task, args[2])
        elif name == "OP":
            outer_pack()
            outer_pair()
        elif name == "OL":
            outer_line()
        elif name == "OF":
            outer_finish()
        elif name == "PG":
            prep_gain()
        elif name == "PD":
            prep_down()
        elif name == "PU":
            prep_gate_up()
        elif name == "SQ":
            add_squares(task)
        elif name == "FW":
            if args[0] == 0:
                inverse_scale()
            forward(4 * args[0], 4 * args[0] + 4)
        elif name == "BW":
            backward(task)

    for i, op in enumerate(ORDER):
        if i == 3:
            for load in loads:
                load.start()
        run(op)
    finish()
    for key, copy in started.items():
        if key not in sent:
            copy.wait_send()


CHUNKS = 8


def finish_kernel(
    d_ref, normed_ref, total_ref, mom_ref, anchor_ref,
    grad_gate, grad_up, new_mom, new_anchor,
    gate_v, up_v, out_sem,
):
    wide = D // CHUNKS
    writes = []
    for c in range(CHUNKS):
        cols = pl.ds(c * wide, wide)
        out = lax.dot_general(d_ref[...], normed_ref[:, cols], NN, preferred_element_type=F32)
        gate_v[:, cols] = out[:HID].astype(BF16)
        up_v[:, cols] = out[HID:].astype(BF16)
        for i, (src, dst) in enumerate(((gate_v, grad_gate), (up_v, grad_up))):
            writes.append(
                pltpu.make_async_copy(src.at[:, cols], dst.at[:, cols], out_sem.at[c, i])
            )
            writes[-1].start()
    mean_delta = total_ref[:11] / 8.0
    momentum = outer_beta * mom_ref[...] + mean_delta
    new_mom[...] = momentum
    new_anchor[...] = (
        anchor_ref[...].astype(F32) - outer_rate * (mean_delta + outer_beta * momentum)
    ).astype(BF16)
    for write in writes:
        write.wait()


def body(
    tokens, norm_gain, gate_weight, up_weight, down_weight, cotangent, outer_delta, momentum, anchor
):
    vmem = pl.BlockSpec(memory_space=pltpu.VMEM)
    hbm = pl.BlockSpec(memory_space=pltpu.HBM)
    dma = pltpu.SemaphoreType.DMA
    d_t, normed, total = pl.pallas_call(
        kernel,
        out_shape=(
            pltpu.VMEM((2 * HID, 512), BF16),
            pltpu.VMEM((512, D), BF16),
            pltpu.VMEM((16, D), F32),
        ),
        in_specs=[hbm] * 7,
        out_specs=(vmem, vmem, vmem),
        scratch_shapes=[
            pltpu.VMEM((2, 2, 4, 4, 4, 64, 256), BF16),
            pltpu.VMEM((HID, D), BF16),
            pltpu.VMEM((HID, D), BF16),
            pltpu.VMEM((HID, D), BF16),
            pltpu.VMEM((HID, D), BF16),
            pltpu.VMEM((2 * HID, D), BF16),
            pltpu.VMEM((4, 4, HID, 256), BF16),
            pltpu.VMEM((2 * HID, 512), F32),
            pltpu.VMEM((HID, 512), F32),
            pltpu.VMEM((8, 512), F32),
            pltpu.VMEM((D, 128), F32),
            pltpu.VMEM((32, 128), BF16),
            pltpu.VMEM((2, 4, 16, D), BF16),
            pltpu.VMEM((4, 16, D), BF16),
            pltpu.VMEM((4, 16, D), BF16),
            pltpu.VMEM((3, 16, D), BF16),
            dma((5,)),
            dma((2, 2)),
            dma((2, 2, 4, COPIES)),
            dma((2, 2, 4, COPIES)),
            dma((2, 2, 3)),
            dma((2, 2, 3)),
            dma((4,)),
            dma((4,)),
        ],
        compiler_params=pltpu.CompilerParams(
            collective_id=0, has_side_effects=True, vmem_limit_bytes=48 * 2**20
        ),
        cost_estimate=pl.CostEstimate(
            flops=6 * 512 * D * HID, bytes_accessed=8 * 2**20, transcendentals=512 * HID
        ),
        name="gather_and_forward",
    )(
        *(
            pltpu.with_memory_space_constraint(a, pltpu.HBM)
            for a in (
                tokens.T, cotangent.T, norm_gain.reshape(32, 128), gate_weight[0], up_weight[0], down_weight[0],
                outer_delta[0],
            )
        )
    )
    d_t, normed, total = (
        pltpu.with_memory_space_constraint(a, pltpu.VMEM) for a in (d_t, normed, total)
    )
    outs = pl.pallas_call(
        finish_kernel,
        out_shape=(
            jax.ShapeDtypeStruct((HID, D), BF16),
            jax.ShapeDtypeStruct((HID, D), BF16),
            jax.ShapeDtypeStruct((11, D), F32),
            jax.ShapeDtypeStruct((11, D), BF16),
        ),
        in_specs=[vmem, vmem, vmem, vmem, vmem],
        out_specs=(hbm, hbm, vmem, vmem),
        scratch_shapes=[
            pltpu.VMEM((HID, D), BF16),
            pltpu.VMEM((HID, D), BF16),
            dma((CHUNKS, 2)),
        ],
        compiler_params=pltpu.CompilerParams(vmem_limit_bytes=16 * 2**20),
        cost_estimate=pl.CostEstimate(
            flops=4 * 512 * D * HID, bytes_accessed=6 * 2**20, transcendentals=0
        ),
        name="gradients_and_outer_update",
    )(d_t, normed, total, momentum, anchor)
    return outs[0][None], outs[1][None], outs[2], outs[3]


def solution(mesh):
    return jax.shard_map(
        body,
        mesh=mesh,
        in_specs=(
            P("rep", "fsdp"),
            P(),
            P("rep", "fsdp", None),
            P("rep", "fsdp", None),
            P("rep", "fsdp", None),
            P("rep", "fsdp"),
            P("rep", "fsdp", None),
            P(("fsdp", "rep"), None),
            P(("fsdp", "rep"), None),
        ),
        out_specs=(
            P("rep", "fsdp", None),
            P("rep", "fsdp", None),
            P(("fsdp", "rep"), None),
            P(("fsdp", "rep"), None),
        ),
        check_vma=False,
    )
```

```python
import functools

import jax
import jax.numpy as jnp
from jax import lax
from jax.experimental import pallas as pl
from jax.experimental.pallas import tpu as pltpu
from jax.sharding import PartitionSpec as P

norm_epsilon = 1e-06
outer_beta = 0.9
outer_rate = 0.7

MESH = pl.DeviceIdType.MESH
F32 = jnp.float32
BF16 = jnp.bfloat16
D = 4096
HID = 88
NT = (((1,), (1,)), ((), ()))
NN = (((1,), (0,)), ((), ()))
TOK, COT = 0, 1
DIRECT = ((TOK, 0), (COT, 0))
ORDER = (
    ('Z', 0), ('F', 0, 0), ('Z', 1), ('F', 1, 0), ('S', 0, 0, 0), ('S', 1, 0, 0), ('PG',), ('OP',),
    ('S', 0, 0, 1), ('PU',), ('S', 1, 0, 1), ('SF', 1, 0, 0), ('SF', 0, 0, 0), ('ZF', 0), ('S', 0, 1, 0),
    ('F', 0, 1), ('F', 0, 3), ('S', 0, 3, 0), ('SF', 1, 0, 1), ('SF', 0, 0, 1), ('FF', 0, 1), ('SF', 0, 1, 0),
    ('FF', 0, 3), ('SF', 0, 3, 0), ('S', 1, 3, 0), ('ZF', 1), ('F', 1, 3), ('F', 1, 1), ('S', 0, 1, 1),
    ('F', 0, 2), ('S', 1, 1, 0), ('S', 0, 3, 1), ('PD',), ('SQ', 0, 0), ('OL',), ('FF', 1, 3), ('FF', 1, 1),
    ('FF', 0, 2), ('S', 0, 2, 0), ('F', 1, 2), ('SF', 0, 1, 1), ('SF', 0, 3, 1), ('BW', 1, 0), ('S', 0, 2, 1),
    ('SF', 0, 2, 0), ('FF', 1, 2), ('S', 1, 2, 0), ('S', 1, 3, 1), ('SF', 0, 2, 1), ('S', 1, 1, 1),
    ('S', 1, 2, 1), ('SQ', 0, 3), ('SF', 1, 3, 1), ('SQ', 0, 2), ('SQ', 0, 1), ('SF', 1, 3, 0),
    ('SF', 1, 1, 0), ('SF', 1, 2, 0), ('FW', 0), ('SF', 1, 1, 1), ('FW', 1), ('SF', 1, 2, 1), ('OF',),
    ('FW', 2), ('FW', 3), ('BW', 1, 3), ('BW', 1, 1), ('BW', 1, 2),
)
GROUPS = {
    (0, 0): ((0, 1), (1, 4)),
    (1, 0): ((0, 1), (1, 4)),
    (0, 3): ((0, 1), (1, 4)),
    (0, 1): ((0, 1), (1, 4)),
    (1, 3): ((0, 1), (1, 4)),
    (0, 2): ((0, 1), (1, 4)),
    (1, 1): ((0, 1), (1, 4)),
    (1, 2): ((0, 1), (1, 4)),
}
COPIES = 4 + 4 * max(len(groups) for groups in GROUPS.values())


def kernel(
    tok_hbm, cot_hbm, gain_hbm, gate_hbm, up_hbm, down_hbm, delta_hbm,
    d_out, normed, total_out,
    g, gate_w, up_w, down_w, delta_v, gate_up, down_z, acc_pre, acc_back, squares, gain_v, gain_ref,
    share, pair_in, pair_out, line_in,
    load_sem, own_sem, send, recv, zsend, zrecv, osend, orecv,
):
    f = lax.axis_index("fsdp")
    r = lax.axis_index("rep")
    y, x, zh = f // 16, (f // 4) % 4, f % 4
    zl, core = r // 2, r % 2

    def at(yy, xx, zz):
        return {"fsdp": ((yy + 4) % 4) * 16 + ((xx + 4) % 4) * 4 + (zz + 4) % 4}

    xn = (at(y, x + 1, zh), at(y, x - 1, zh), at(y, x + 2, zh))
    yn = (at(y + 1, x, zh), at(y - 1, x, zh), at(y + 2, x, zh))
    zn = (at(y, x, zh + 1), at(y, x, zh - 1))
    partner = {"rep": zl * 2 + 1 - core}
    line = [{"rep": ((zl + k) % 4) * 2 + core} for k in (1, 2, 3)]

    def mine(t, h):
        return (tok_hbm, cot_hbm)[t].at[:, pl.ds(256 * h, 256)]

    own = [
        pltpu.make_async_copy(mine(t, h), g.at[t, h, 0, 0, 0], own_sem.at[t, h])
        for t in (TOK, COT)
        for h in range(2)
    ]
    loads = [
        pltpu.make_async_copy(src, dst, load_sem.at[i])
        for i, (src, dst) in enumerate(
            ((delta_hbm, delta_v), (gate_hbm, gate_w), (up_hbm, up_w), (down_hbm, down_w), (gain_hbm, gain_ref))
        )
    ]
    barrier = pltpu.get_barrier_semaphore()
    peers = [*xn, *yn, *zn, *line, partner]
    for i, peer in enumerate(peers):
        pl.semaphore_signal(barrier, inc=1, device_id=peer, device_id_type=MESH)
        if i == 5:
            for load in own:
                load.start()
    for load in own:
        load.wait()
    pl.semaphore_wait(barrier, len(peers))

    started, arrived = {}, set()

    def start(key, src, dst, ssem, rsem, device):
        copy = pltpu.make_async_remote_copy(
            src_ref=src, dst_ref=dst, send_sem=ssem, recv_sem=rsem,
            device_id=device, device_id_type=MESH,
        )
        copy.start()
        started[key] = copy

    def need(key):
        if key not in arrived:
            arrived.add(key)
            started[key].wait_recv()

    def xy(task, h, k, src, dst, device):
        t, rz = task
        start((task, h, k), src, dst, send.at[t, h, rz, k], recv.at[t, h, rz, k], device)

    def near(h):
        return (xn, yn) if h == 0 else (yn, xn)

    lo, hi = pl.ds(0, 32), pl.ds(32, 32)

    def first_send(task):
        for h in range(2):
            b = g.at[task[0], h, task[1]]
            src = b.at[0, 0]
            xy(task, h, 0, src, b.at[0, 3], near(h)[0][0])
            xy(task, h, 1, src, b.at[0, 1], near(h)[0][1])
            if task in DIRECT:
                xy(task, h, 2, src, b.at[0, 2], near(h)[0][2])

    def first_forward(task):
        if task in DIRECT:
            return
        for h in range(2):
            b = g.at[task[0], h, task[1]]
            need((task, h, 0))
            xy(task, h, 2, b.at[0, 3, lo], b.at[0, 2, lo], near(h)[0][0])
            need((task, h, 1))
            xy(task, h, 3, b.at[0, 1, hi], b.at[0, 2, hi], near(h)[0][1])

    brings = {0: (), 1: (1,), 2: (2, 3), 3: (0,)}

    def second_send(task, i):
        first, last = GROUPS[task][i]
        for h in range(2):
            b = g.at[task[0], h, task[1]]
            for offset in range(first, last):
                for k in (2,) if task in DIRECT and offset == 2 else brings[offset]:
                    need((task, h, k))
            cols = pl.ds(first, last - first)
            src = b.at[0, cols]
            xy(task, h, 4 + 4 * i, src, b.at[3, cols], near(h)[1][0])
            xy(task, h, 5 + 4 * i, src, b.at[1, cols], near(h)[1][1])

    def second_forward(task, i):
        first, last = GROUPS[task][i]
        for h in range(2):
            b = g.at[task[0], h, task[1]]
            cols = pl.ds(first, last - first)
            need((task, h, 4 + 4 * i))
            xy(task, h, 6 + 4 * i, b.at[3, cols, lo], b.at[2, cols, lo], near(h)[1][0])
            need((task, h, 5 + 4 * i))
            xy(task, h, 7 + 4 * i, b.at[1, cols, hi], b.at[2, cols, hi], near(h)[1][1])

    def z_send(t):
        for h in range(2):
            start(("z", t, h, 0), g.at[t, h, 0, 0, 0], g.at[t, h, 3, 0, 0],
                  zsend.at[t, h, 0], zrecv.at[t, h, 0], zn[0])
        for h in (1, 0):
            start(("z", t, h, 1), g.at[t, h, 0, 0, 0], g.at[t, h, 1, 0, 0],
                  zsend.at[t, h, 1], zrecv.at[t, h, 1], zn[1])

    def z_forward(t):
        need(("z", t, 0, 0))
        start(("z", t, 0, 2), g.at[t, 0, 3, 0, 0], g.at[t, 0, 2, 0, 0],
              zsend.at[t, 0, 2], zrecv.at[t, 0, 2], zn[0])
        need(("z", t, 1, 1))
        start(("z", t, 1, 2), g.at[t, 1, 1, 0, 0], g.at[t, 1, 2, 0, 0],
              zsend.at[t, 1, 2], zrecv.at[t, 1, 2], zn[1])

    def z_need(task):
        t, rz = task
        if rz:
            for h in range(2):
                need(("z", t, h, {3: 0, 1: 1, 2: 2}[rz]))

    sent = set()

    def arrive(task):
        for h in range(2):
            for i in range(len(GROUPS[task])):
                need((task, h, 6 + 4 * i))
                need((task, h, 7 + 4 * i))
        for key, copy in started.items():
            if key[0] == task and key not in sent:
                sent.add(key)
                copy.wait_send()

    def outer_pack():
        loads[0].wait()

        @pl.loop(0, 8)
        def _(c):
            cols = pl.ds(pl.multiple_of(c * 512, 512), 512)
            rows = delta_v[:, cols].astype(F32)
            for b in range(8):
                if b < 7:
                    block = rows[b * 11 : b * 11 + 16]
                else:
                    block = jnp.concatenate([rows[77:88], jnp.zeros((5, 512), F32)], axis=0)
                share[b % 2, b // 2, :, cols] = block.astype(BF16)

    def outer_pair():
        start("pair", share.at[1 - core], pair_in, osend.at[0], orecv.at[0], partner)

    def outer_line():
        need("pair")

        @pl.loop(0, 4)
        def _(b):
            pair_out[b] = (share[core, b].astype(F32) + pair_in[b].astype(F32)).astype(BF16)

        for k in range(3):
            start(("line", k), pair_out.at[(zl + k + 1) % 4], line_in.at[k],
                  osend.at[1 + k], orecv.at[1 + k], line[k])

    def outer_finish():
        for k in range(3):
            need(("line", k))
        total = share[core, zl].astype(F32) + pair_in[zl].astype(F32)
        for k in range(3):
            total = total + line_in[k].astype(F32)
        total_out[...] = total

    def prep_gate_up():
        loads[1].wait()
        loads[2].wait()

        @pl.loop(0, 8)
        def _(c):
            cols = pl.ds(pl.multiple_of(c * 512, 512), 512)
            gate_up[:, cols] = jnp.concatenate(
                [gate_w[:, cols].astype(F32), up_w[:, cols].astype(F32)], axis=0
            ).astype(BF16)

    def prep_gain():
        loads[4].wait()

        rows = gain_ref[...].astype(F32)
        for c in range(32):
            gain_v[c * 128 : c * 128 + 128, :] = jnp.broadcast_to(rows[c : c + 1], (128, 128)).T

        acc_back[...] = jnp.zeros_like(acc_back)
        acc_pre[...] = jnp.zeros_like(acc_pre)
        squares[...] = jnp.zeros_like(squares)

    def prep_down():
        loads[3].wait()
        low = lax.broadcasted_iota(jnp.int32, (HID, 128), 1) < 64

        @pl.loop(0, 4)
        def _(yy):
            for pair in range(2):
                for xs in range(2):
                    a, b = (
                        down_w[
                            :, pl.ds(pl.multiple_of((yy * 4 + xx) * 256 + pair * 128, 128), 128)
                        ].astype(F32)
                        for xx in (2 * xs, 2 * xs + 1)
                    )
                    lanes = pl.ds(xs * 128, 128)
                    down_z[2 * pair, yy, :, lanes] = jnp.where(low, a, pltpu.roll(b, 64, 1)).astype(BF16)
                    down_z[2 * pair + 1, yy, :, lanes] = jnp.where(low, pltpu.roll(a, 64, 1), b).astype(BF16)

    def block_of(t, rz, ry, rx):
        return jnp.concatenate([g[t, 0, rz, ry, rx], g[t, 1, rz, rx, ry]], axis=1)

    def add_squares(task):
        arrive(task)

        @pl.loop(0, 16, unroll=2)
        def _(b):
            v = block_of(TOK, task[1], b // 4, b % 4).astype(F32)
            v = v * v
            part = v[:8]
            for i in range(1, 8):
                part = part + v[8 * i : 8 * i + 8]
            squares[...] += part

    def inverse_scale():
        total = jnp.sum(squares[...], axis=0, keepdims=True)
        squares[...] = jnp.broadcast_to(1.0 / jnp.sqrt(total / D + norm_epsilon), squares.shape)

    def forward(first, last):
        @pl.loop(first, last, unroll=2)
        def _(b):
            ry, rx = (b // 4 - y + 4) % 4, (b % 4 - x + 4) % 4
            cols = pl.ds(pl.multiple_of(b * 256, 256), 256)
            scale = squares[0:1, :]
            gain = gain_v[cols, :]
            gain = jnp.concatenate([gain] * 4, axis=1)
            raw = jnp.concatenate(
                [block_of(TOK, (zs - zh + 4) % 4, ry, rx) for zs in range(4)], axis=0
            )
            block = (raw.astype(F32) * scale * gain).astype(BF16)
            normed[:, cols] = block.T
            acc_pre[...] += lax.dot_general(
                gate_up[:, cols], block, NN, preferred_element_type=F32
            )

    def backward(task):
        arrive(task)
        rz = task[1]
        zs = (zh + rz) % 4

        @pl.loop(0, 4, unroll=4)
        def _(yy):
            ry = (yy - y + 4) % 4
            rows = jnp.concatenate(
                [block_of(COT, rz, ry, (xx - x + 4) % 4) for xx in range(4)], axis=0
            )
            acc_back[...] += lax.dot_general(
                down_z[zs, yy], rows, NN, preferred_element_type=F32
            )

    def finish():
        for q in range(4):
            lanes = pl.ds(q * 128, 128)
            gate_pre = acc_pre[:HID, lanes]
            up_pre = acc_pre[HID:, lanes]
            back = acc_back[:, lanes]
            sig = jax.nn.sigmoid(gate_pre)
            d_gate = back * up_pre * sig * (1.0 + gate_pre * (1.0 - sig))
            d_up = back * gate_pre * sig
            d_out[:, lanes] = jnp.concatenate([d_gate, d_up], axis=0).astype(BF16)

    def run(op):
        name, args = op[0], op[1:]
        task = args[:2]
        if name == "Z":
            z_send(args[0])
        elif name == "ZF":
            z_forward(args[0])
        elif name == "F":
            z_need(task)
            first_send(task)
        elif name == "FF":
            first_forward(task)
        elif name == "S":
            z_need(task)
            second_send(task, args[2])
        elif name == "SF":
            second_forward(task, args[2])
        elif name == "OP":
            outer_pack()
            outer_pair()
        elif name == "OL":
            outer_line()
        elif name == "OF":
            outer_finish()
        elif name == "PG":
            prep_gain()
        elif name == "PD":
            prep_down()
        elif name == "PU":
            prep_gate_up()
        elif name == "SQ":
            add_squares(task)
        elif name == "FW":
            if args[0] == 0:
                inverse_scale()
            forward(4 * args[0], 4 * args[0] + 4)
        elif name == "BW":
            backward(task)

    for i, op in enumerate(ORDER):
        if i == 3:
            for load in loads:
                load.start()
        run(op)
    finish()
    for key, copy in started.items():
        if key not in sent:
            copy.wait_send()


CHUNKS = 8


def finish_kernel(
    d_ref, normed_ref, total_ref, mom_ref, anchor_ref,
    grad_gate, grad_up, new_mom, new_anchor,
    gate_v, up_v, out_sem,
):
    wide = D // CHUNKS
    writes = []
    for c in range(CHUNKS):
        cols = pl.ds(c * wide, wide)
        out = lax.dot_general(d_ref[...], normed_ref[:, cols], NN, preferred_element_type=F32)
        gate_v[:, cols] = out[:HID].astype(BF16)
        up_v[:, cols] = out[HID:].astype(BF16)
        for i, (src, dst) in enumerate(((gate_v, grad_gate), (up_v, grad_up))):
            writes.append(
                pltpu.make_async_copy(src.at[:, cols], dst.at[:, cols], out_sem.at[c, i])
            )
            writes[-1].start()
    mean_delta = total_ref[:11] / 8.0
    momentum = outer_beta * mom_ref[...] + mean_delta
    new_mom[...] = momentum
    new_anchor[...] = (
        anchor_ref[...].astype(F32) - outer_rate * (mean_delta + outer_beta * momentum)
    ).astype(BF16)
    for write in writes:
        write.wait()


def body(
    tokens, norm_gain, gate_weight, up_weight, down_weight, cotangent, outer_delta, momentum, anchor
):
    vmem = pl.BlockSpec(memory_space=pltpu.VMEM)
    hbm = pl.BlockSpec(memory_space=pltpu.HBM)
    dma = pltpu.SemaphoreType.DMA
    d_t, normed, total = pl.pallas_call(
        kernel,
        out_shape=(
            pltpu.VMEM((2 * HID, 512), BF16),
            pltpu.VMEM((512, D), BF16),
            pltpu.VMEM((16, D), F32),
        ),
        in_specs=[hbm] * 7,
        out_specs=(vmem, vmem, vmem),
        scratch_shapes=[
            pltpu.VMEM((2, 2, 4, 4, 4, 64, 256), BF16),
            pltpu.VMEM((HID, D), BF16),
            pltpu.VMEM((HID, D), BF16),
            pltpu.VMEM((HID, D), BF16),
            pltpu.VMEM((HID, D), BF16),
            pltpu.VMEM((2 * HID, D), BF16),
            pltpu.VMEM((4, 4, HID, 256), BF16),
            pltpu.VMEM((2 * HID, 512), F32),
            pltpu.VMEM((HID, 512), F32),
            pltpu.VMEM((8, 512), F32),
            pltpu.VMEM((D, 128), F32),
            pltpu.VMEM((32, 128), BF16),
            pltpu.VMEM((2, 4, 16, D), BF16),
            pltpu.VMEM((4, 16, D), BF16),
            pltpu.VMEM((4, 16, D), BF16),
            pltpu.VMEM((3, 16, D), BF16),
            dma((5,)),
            dma((2, 2)),
            dma((2, 2, 4, COPIES)),
            dma((2, 2, 4, COPIES)),
            dma((2, 2, 3)),
            dma((2, 2, 3)),
            dma((4,)),
            dma((4,)),
        ],
        compiler_params=pltpu.CompilerParams(
            collective_id=0, has_side_effects=True, vmem_limit_bytes=48 * 2**20
        ),
        cost_estimate=pl.CostEstimate(
            flops=6 * 512 * D * HID, bytes_accessed=8 * 2**20, transcendentals=512 * HID
        ),
        name="gather_and_forward",
    )(
        *(
            pltpu.with_memory_space_constraint(a, pltpu.HBM)
            for a in (
                tokens.T, cotangent.T, norm_gain.reshape(32, 128), gate_weight[0], up_weight[0], down_weight[0],
                outer_delta[0],
            )
        )
    )
    d_t, normed, total = (
        pltpu.with_memory_space_constraint(a, pltpu.VMEM) for a in (d_t, normed, total)
    )
    outs = pl.pallas_call(
        finish_kernel,
        out_shape=(
            jax.ShapeDtypeStruct((HID, D), BF16),
            jax.ShapeDtypeStruct((HID, D), BF16),
            jax.ShapeDtypeStruct((11, D), F32),
            jax.ShapeDtypeStruct((11, D), BF16),
        ),
        in_specs=[vmem, vmem, vmem, vmem, vmem],
        out_specs=(hbm, hbm, vmem, vmem),
        scratch_shapes=[
            pltpu.VMEM((HID, D), BF16),
            pltpu.VMEM((HID, D), BF16),
            dma((CHUNKS, 2)),
        ],
        compiler_params=pltpu.CompilerParams(vmem_limit_bytes=16 * 2**20),
        cost_estimate=pl.CostEstimate(
            flops=4 * 512 * D * HID, bytes_accessed=6 * 2**20, transcendentals=0
        ),
        name="gradients_and_outer_update",
    )(d_t, normed, total, momentum, anchor)
    return outs[0][None], outs[1][None], outs[2], outs[3]


def solution(mesh):
    return jax.shard_map(
        body,
        mesh=mesh,
        in_specs=(
            P("rep", "fsdp"),
            P(),
            P("rep", "fsdp", None),
            P("rep", "fsdp", None),
            P("rep", "fsdp", None),
            P("rep", "fsdp"),
            P("rep", "fsdp", None),
            P(("fsdp", "rep"), None),
            P(("fsdp", "rep"), None),
        ),
        out_specs=(
            P("rep", "fsdp", None),
            P("rep", "fsdp", None),
            P(("fsdp", "rep"), None),
            P(("fsdp", "rep"), None),
        ),
        check_vma=False,
    )
```
